256 devices in a mesh: grp: 8 (over y_hi, x), blk: 32 (over y_lo, z, core).
Axes of the slice: x: 4, y: 4 (y_hi: 2, y_lo: 2; y = y_hi * 2 + y_lo), z: 8, core: 2. Of those that a mesh axis runs over, the one named last changes fastest.
Arguments:
- voltages: bfloat16 [4096, 188416], P(('blk', 'grp')), may hold values from -6 to 6
- filter_taps: float32 [8, 8192], replicated, may hold values from -0.0234375 to 0.0234375
- channel_index: int32 [16], replicated, may hold values from 0 to 4095
- antenna_slot_order: int32 [2048], replicated, may hold values from 0 to 2047, each once
Outputs:
- visibilities: bfloat16 [16, 4096, 2, 4096], P('grp', 'blk')
The draws below stay inside these ranges and needn't reach their ends.
All inputs are finite; a program needn't handle non-finite values.
Results may differ from the reference program's by a relative error of at most 0.0065.
Values sent between devices are 32-bit elements; how exact they have to be, the bound alone decides.
A program may use at most 64 MiB of HBM per device.

```python
import math
import jax
import jax.numpy as jnp
from jax import lax

ANTENNA_COUNT = 2048
NFFT = 8192
TAPS = 8
CH = 16
SPEC = 16
INPUTS = 4096
SAMPLES = 188416


def with_ends(result, key, smallest, high):
    longest = result.shape.index(max(result.shape))
    spots = []
    for shift in (0, 1):
        where = [jax.random.randint(jax.random.fold_in(key, axis), (), 0, length) for axis, length in enumerate(result.shape)]
        where[longest] = (where[longest] + shift) % result.shape[longest]
        spots.append(tuple(where))
    return result.at[spots[0]].set(smallest).at[spots[1]].set(high)


def steps_of(rng, shape, cuts, smallest, largest):
    def one(dim, shards_of):
        steps = jax.random.uniform(jax.random.fold_in(jax.random.fold_in(rng, 6), dim), (shards_of,), jnp.float32, smallest / len(cuts), largest / len(cuts))
        return jnp.repeat(jnp.exp(steps), shape[dim] // shards_of).reshape((-1,) + (1,) * (len(shape) - dim - 1))

    loudness = one(*cuts[0])
    for cut in cuts[1:]:
        loudness = loudness * one(*cut)
    return loudness


def bell_draw(rng, dims, scale, most, shards=(), held_as=jnp.bfloat16):
    result = jax.random.normal(rng, dims, jnp.float32) * scale
    if len(shards) > 0:
        result = steps_of(rng, dims, shards, -0.22, 0.18) * result
    return jnp.clip(result, min=-most, max=most).astype(held_as)


def setup_inputs(seed: int = 0) -> dict:
    key_list = jax.random.split(jax.random.key(seed), 5)
    return {
        "voltages": bell_draw(key_list[0], (INPUTS, SAMPLES), 1.0, 6.0, ((0, 256),)),
        "filter_taps": bell_draw(key_list[1], (TAPS, NFFT), (TAPS * NFFT) ** -0.5, 0.0234375, (), jnp.float32),
        "channel_index": with_ends(jax.random.randint(key_list[2], (CH,), 0, NFFT // 2), jax.random.fold_in(key_list[2], 1), 0, (NFFT // 2) - 1).astype(jnp.int32),
        "antenna_slot_order": jax.random.permutation(key_list[3], ANTENNA_COUNT).astype(jnp.int32),
    }


def phase_table(channel_index, fft_length):
    samples_idx = jnp.arange(fft_length, dtype=jnp.int32)
    phase = (samples_idx[:, None] * channel_index[None, :].astype(jnp.int32)) % fft_length
    angle = phase.astype(jnp.float32) * jnp.float32(2.0 * math.pi / fft_length)
    return jnp.concatenate([jnp.cos(angle), -jnp.sin(angle)], axis=1).astype(jnp.bfloat16)


def channelize(voltages, filter_taps, channel_index):
    tap_count, fft_length = filter_taps.shape
    row_count = voltages.shape[0]
    frame_count = voltages.shape[1] // fft_length
    spectra = frame_count - tap_count + 1
    blocked = voltages.reshape(row_count, frame_count, fft_length)
    filtered = jnp.zeros((row_count, spectra, fft_length), jnp.float32)
    for tap_index in range(tap_count):
        filtered = filtered + filter_taps[tap_index][None, None, :] * blocked[:, tap_index:tap_index + spectra, :].astype(jnp.float32)
    twiddle = phase_table(channel_index, fft_length)
    spectrum = jnp.dot(filtered.astype(jnp.bfloat16).reshape(row_count * spectra, fft_length), twiddle, preferred_element_type=jnp.float32)
    chan_count = channel_index.shape[0]
    return spectrum.reshape(row_count, spectra, 2, chan_count).transpose(3, 2, 1, 0).reshape(chan_count, 2 * spectra, row_count)


def column_index(antenna_slot_order):
    count = antenna_slot_order.shape[0]
    inverse = jnp.zeros((count,), jnp.int32).at[antenna_slot_order].set(jnp.arange(count, dtype=jnp.int32))
    column_entry = jnp.arange(2 * count, dtype=jnp.int32)
    return 2 * inverse[column_entry // 2] + column_entry % 2


def stacked_rows(block):
    half = block.shape[1] // 2
    turned = jnp.concatenate([block[:, half:], -block[:, :half]], axis=1)
    return jnp.stack([block, turned], axis=1)


def reference(voltages, filter_taps, channel_index, antenna_slot_order):
    rows_per_block = 128 if INPUTS % 128 == 0 else INPUTS
    grouped_rows = voltages.reshape(INPUTS // rows_per_block, rows_per_block, SAMPLES)
    pieces = lax.map(lambda part_rows: channelize(part_rows, filter_taps, channel_index), grouped_rows)
    spectra_all = jnp.moveaxis(pieces, 0, 2).reshape(CH, 2 * SPEC, INPUTS)
    columns = column_index(antenna_slot_order)
    ordered = jnp.take(spectra_all, columns, axis=2)
    lhs_all = stacked_rows(spectra_all)
    scale = jnp.float32(1.0 / SPEC)

    def one_channel(pair):
        left_operand_single, cols_one = pair
        product = jnp.einsum("pkr,kn->rpn", left_operand_single, cols_one, precision=lax.Precision.HIGHEST, preferred_element_type=jnp.float32)
        return (product * scale).astype(jnp.bfloat16)

    return lax.map(one_channel, (lhs_all, ordered))
```

```python
import functools
import math

import jax
import jax.numpy as jnp
from jax import lax
from jax.experimental import pallas as pl
from jax.experimental.pallas import tpu as pltpu
from jax.sharding import PartitionSpec as P

F32, BF16, I32 = jnp.float32, jnp.bfloat16, jnp.int32
MESH = pl.DeviceIdType.MESH
NFFT, TAPS, SPEC, FRAMES = 8192, 8, 16, 23
CHUNKS = 4
WIDTH = NFFT // CHUNKS
FORM = 1024
QBLOCK = 512


def iota(shape, dim):
    return lax.broadcasted_iota(I32, shape, dim)


def form_weights(index_ref, taps_ref, weights):
    shape = (32, 128)
    row, lane = iota(shape, 0), iota(shape, 1)
    channel = jnp.zeros(shape, I32)
    for c in range(16):
        channel = jnp.where(row >> 1 == c, index_ref[c], channel)
    real = (row & 1) == 0
    unit = jnp.float32(2.0 * math.pi / NFFT)
    fine = ((lane * channel) & (NFFT - 1)).astype(F32) * unit
    coarse = (((lane * channel) & 63) * 128).astype(F32) * unit
    cos_fine, sin_fine = jnp.cos(fine), jnp.sin(fine)
    cos_coarse, sin_coarse = jnp.cos(coarse), jnp.sin(coarse)
    first = jnp.where(real, cos_fine, -sin_fine)
    second = jnp.where(real, -sin_fine, -cos_fine)
    per = FORM // 128

    def step(i, _):
        shift = (128 - i * per) % 128
        cos_here = pltpu.roll(cos_coarse, shift, 1)
        sin_here = pltpu.roll(sin_coarse, shift, 1)
        for j in range(per):
            at = pl.ds(pl.multiple_of(i * FORM + j * 128, 128), 128)
            cos_b = jnp.broadcast_to(cos_here[:, j : j + 1], shape)
            sin_b = jnp.broadcast_to(sin_here[:, j : j + 1], shape)
            twiddle = (first * cos_b + second * sin_b).astype(BF16).astype(F32)
            for m in range(TAPS):
                weights[pl.ds(m * 32, 32), at] = (
                    taps_ref[pl.ds(m, 1), at] * twiddle
                ).astype(BF16)
        return _

    lax.fori_loop(0, NFFT // FORM, step, 0)


def channelize(index_ref, taps_ref, volts, volts_sem, weights, acc):
    form_weights(index_ref, taps_ref, weights)
    for c in range(CHUNKS):
        pltpu.make_async_copy(volts.at[c], volts.at[c], volts_sem.at[c]).wait()
        part = lax.dot_general(
            volts[c].reshape(FRAMES * 16, WIDTH),
            weights[:, pl.ds(c * WIDTH, WIDTH)],
            (((1,), (1,)), ((), ())),
            preferred_element_type=F32,
        )
        if c == 0:
            acc[...] = part
        else:
            acc[...] += part


def pieces_of(acc, pairs, pieces):
    lane = iota((16, 128), 1)
    group = lane >> 2
    sums = [
        acc[pl.ds(f * 16, 16), :128] + acc[pl.ds((f + 4) * 16, 16), 128:]
        for f in range(SPEC + 3)
    ]
    spectra = []
    for t in range(SPEC):
        x = sums[t + 3]
        for j in (2, 1, 0):
            x = jnp.where(lane < 32 * (j + 1), sums[t + j], x)
        x = x + pltpu.roll(x, 64, 1)
        spectra.append(x + pltpu.roll(x, 32, 1))
    turned = []
    for s in range(8):
        x = spectra[s]
        for q in range(1, 16):
            x = jnp.where((group & 15) == q, spectra[(q + s) % 16], x)
        turned.append(pltpu.roll(x, 4 * s, 1) if s else x)
    for g in range(8):
        x = turned[0]
        for s in range(1, 8):
            x = jnp.where(((group - g) & 7) == s, turned[s], x)
        pairs[g] = x
    low = iota((8, 128), 1) < 64
    for g in range(8):
        even = pairs[g, pl.ds(0, 8, stride=2), :]
        odd = pairs[g, pl.ds(1, 8, stride=2), :]
        pieces[g] = jnp.where(low, even, odd)


def spectra_kernel(
    index_ref, taps_ref, volts_hbm, out_ref,
    volts, weights, acc, pairs, pieces, buf,
    volts_sem, a_send, a_recv, z_send, z_recv, y_send, y_recv, c_send, c_recv,
):
    grp, blk = lax.axis_index("grp"), lax.axis_index("blk")
    yh, x = grp // 4, grp % 4
    yl, z, core = blk // 16, (blk // 2) % 8, blk % 2

    def start(c, _):
        for f in range(FRAMES):
            at = pl.ds(pl.multiple_of(f * NFFT + c * WIDTH, 128), WIDTH)
            pltpu.make_async_copy(
                volts_hbm.at[:, at], volts.at[c, f], volts_sem.at[c]
            ).start()
        return _

    lax.fori_loop(0, CHUNKS, start, 0)

    def at_grp(i, j):
        return ((yh + i) % 2 * 4 + (x + j) % 4, blk)

    def at_z(d):
        return (grp, (yl * 8 + (z + d) % 8) * 2 + core)

    others = [(i, j) for i in range(2) for j in range(4) if (i, j) != (0, 0)]
    y_device = (grp, ((1 - yl) * 8 + z) * 2 + core)
    c_device = (grp, blk + 1 - 2 * core)

    barrier = pltpu.get_barrier_semaphore()
    partners = [at_grp(i, j) for i, j in others] + [at_z(d) for d in range(1, 8)]
    partners += [y_device, c_device]
    for device in partners:
        pl.semaphore_signal(barrier, inc=1, device_id=device, device_id_type=MESH)

    channelize(index_ref, taps_ref, volts, volts_sem, weights, acc)
    pieces_of(acc, pairs, pieces)
    pl.semaphore_wait(barrier, len(partners))

    def send(src, dst, s, r, device):
        copy = pltpu.make_async_remote_copy(
            src_ref=src, dst_ref=dst, send_sem=s, recv_sem=r,
            device_id=device, device_id_type=MESH,
        )
        copy.start()
        sent.append(copy)

    sent = []
    for n, (i, j) in enumerate(sorted(others, key=lambda o: -2 * o[0] - min(o[1], 4 - o[1]))):
        device = at_grp(i, j)
        send(pieces.at[device[0]], buf.at[yl, z, core, grp], a_send.at[n], a_recv.at[n], device)
    buf[yl, z, core, grp] = pieces[grp]
    for copy in sent:
        copy.wait_recv()

    def level(y, d, c):
        return buf.at[y, (z - d + 8) % 8, c]

    arrivals = {}
    for d in (4, 3, 5, 2, 6, 1, 7):
        send(level(yl, 0, core), level(yl, 0, core), z_send.at[d], z_recv.at[d], at_z(d))
        arrivals["z", d] = sent[-1]
    order = (0, 1, 7, 2, 6, 3, 5, 4)

    def from_y(d):
        pltpu.make_async_copy(level(yl, d, core), level(yl, d, core), y_recv.at[d]).wait()
        here = level(1 - yl, d, core)
        send(here, here, c_send.at[8 + d], c_recv.at[8 + d], c_device)

    for n, d in enumerate(order):
        here = level(yl, d, core)
        if d:
            arrivals["z", d].wait_recv()
        send(here, here, y_send.at[d], y_recv.at[d], y_device)
        send(here, here, c_send.at[d], c_recv.at[d], c_device)
        if n >= 2:
            from_y(order[n - 2])
    for d in order[6:]:
        from_y(d)
    for d in range(16):
        here = level(yl, 0, core)
        pltpu.make_async_copy(here, here, c_recv.at[d]).wait()
    for copy in sent:
        copy.wait_send()
    out_ref[...] = buf[...].reshape(out_ref.shape)


def spectra_of_all(index, taps, volts):
    dma = pltpu.SemaphoreType.DMA
    vmem = pltpu.VMEM
    return pl.pallas_call(
        spectra_kernel,
        out_shape=jax.ShapeDtypeStruct((2048, 128), F32),
        in_specs=[
            pl.BlockSpec(memory_space=pltpu.SMEM),
            pl.BlockSpec(memory_space=pltpu.VMEM),
            pl.BlockSpec(memory_space=pl.ANY),
        ],
        out_specs=pl.BlockSpec(memory_space=pltpu.VMEM),
        scratch_shapes=[
            vmem((CHUNKS, FRAMES, 16, WIDTH), BF16),
            vmem((TAPS * 32, NFFT), BF16),
            vmem((FRAMES * 16, TAPS * 32), F32),
            vmem((8, 16, 128), F32),
            vmem((8, 8, 128), F32),
            vmem((2, 8, 2, 8, 8, 128), F32),
            dma((CHUNKS,)), dma((7,)), dma((7,)), dma((8,)), dma((8,)),
            dma((8,)), dma((8,)), dma((16,)), dma((16,)),
        ],
        compiler_params=pltpu.CompilerParams(
            collective_id=0, has_side_effects=True, vmem_limit_bytes=32 << 20
        ),
    )(index, taps, volts)


def prepare(order_ref, all_ref, onehot, permuted, rows, lhs, cols):
    lane = iota((128, 128), 1)

    def chunk(i, _):
        for half in range(2):
            r = i * 2 + half
            slots = order_ref[pl.ds(r, 1), :]
            wide = jnp.broadcast_to(slots.astype(F32), (128, 128)).T.astype(I32)
            for j in range(16):
                onehot[pl.ds(half * 128, 128), pl.ds(j * 128, 128)] = jnp.where(
                    wide == lane + j * 128, 1.0, 0.0
                ).astype(BF16)
        part = lax.dot_general(
            all_ref[pl.ds(pl.multiple_of(i * 256, 256), 256), :].astype(BF16),
            onehot[...],
            (((0,), (0,)), ((), ())),
            preferred_element_type=F32,
        )
        permuted[...] += part
        return _

    permuted[...] = jnp.zeros_like(permuted)
    lax.fori_loop(0, 8, chunk, 0)

    row, col = iota((256, 256), 0), iota((256, 256), 1)
    weave = jnp.where((col >> 1) + (col & 1) * 128 == row, 1.0, 0.0).astype(BF16)
    for j in range(16):
        at = pl.ds(j * 128, 128)
        both = jnp.concatenate([permuted[:64, at], permuted[64:, at]], axis=1)
        cols[:, pl.ds(j * 256, 256)] = jnp.dot(
            both.astype(BF16), weave, preferred_element_type=F32
        ).astype(BF16)

    blk = lax.axis_index("blk")
    mine = all_ref[pl.ds(pl.multiple_of(blk * 64, 64), 64), :] * jnp.float32(1.0 / SPEC)
    even = (iota((64, 128), 1) & 1) == 0
    crossed = jnp.where(even, pltpu.roll(mine, 127, 1), -pltpu.roll(mine, 1, 1))
    for o, part in enumerate((mine, crossed)):
        rows[pl.ds(o, 64, stride=4), :] = part
        rows[pl.ds(2 + o, 64, stride=4), :] = pltpu.roll(part, 64, 1)
    both = rows[...]
    channel = (iota(both.shape, 1) >> 1) & 1
    for c in range(2):
        lhs[c] = jnp.where(channel == c, both, 0.0).astype(BF16)[:, :64]


def correlate_kernel(order_ref, all_ref, out_ref, onehot, permuted, rows, lhs, cols):
    i = pl.program_id(0)

    @pl.when(i == 0)
    def _():
        prepare(order_ref, all_ref, onehot, permuted, rows, lhs, cols)

    right = cols[:, pl.ds(pl.multiple_of(i * QBLOCK, QBLOCK), QBLOCK)]
    for c in range(2):
        x = jnp.dot(lhs[c], right, preferred_element_type=F32)
        out_ref[c] = x.astype(BF16).reshape(128, 2, QBLOCK)


def correlate(order, spectra):
    vmem = pltpu.VMEM
    return pl.pallas_call(
        correlate_kernel,
        grid=(4096 // QBLOCK,),
        out_shape=jax.ShapeDtypeStruct((2, 128, 2, 4096), BF16),
        in_specs=[
            pl.BlockSpec((16, 128), lambda i: (0, 0)),
            pl.BlockSpec((2048, 128), lambda i: (0, 0)),
        ],
        out_specs=pl.BlockSpec((2, 128, 2, QBLOCK), lambda i: (0, 0, 0, i)),
        scratch_shapes=[
            vmem((256, 2048), BF16),
            vmem((128, 2048), F32),
            vmem((256, 128), F32),
            vmem((2, 256, 64), BF16),
            vmem((64, 4096), BF16),
        ],
        compiler_params=pltpu.CompilerParams(vmem_limit_bytes=32 << 20),
    )(order, spectra)


def per_device(voltages, filter_taps, channel_index, antenna_slot_order):
    spectra = spectra_of_all(channel_index, filter_taps, voltages)
    return correlate(antenna_slot_order.reshape(16, 128), spectra)


def solution(mesh):
    in_specs = (P(("blk", "grp"), None), P(), P(), P())
    out_specs = P("grp", "blk", None, None)
    return jax.shard_map(
        per_device, mesh=mesh, in_specs=in_specs, out_specs=out_specs, check_vma=False
    )
```

```python
import functools
import math

import jax
import jax.numpy as jnp
from jax import lax
from jax.experimental import pallas as pl
from jax.experimental.pallas import tpu as pltpu
from jax.sharding import PartitionSpec as P

F32, BF16, I32 = jnp.float32, jnp.bfloat16, jnp.int32
MESH = pl.DeviceIdType.MESH
NFFT, TAPS, SPEC, FRAMES = 8192, 8, 16, 23
WIDTH = 2048
FORM = 1024
QBLOCK = 512


def iota(shape, dim):
    return lax.broadcasted_iota(I32, shape, dim)


def form_weights(index_ref, taps_ref, weights):
    shape = (32, 128)
    row, lane = iota(shape, 0), iota(shape, 1)
    channel = jnp.zeros(shape, I32)
    for c in range(16):
        channel = jnp.where(row >> 1 == c, index_ref[c], channel)
    real = (row & 1) == 0
    unit = jnp.float32(2.0 * math.pi / NFFT)
    fine = ((lane * channel) & (NFFT - 1)).astype(F32) * unit
    coarse = (((lane * channel) & 63) * 128).astype(F32) * unit
    cos_fine, sin_fine = jnp.cos(fine), jnp.sin(fine)
    cos_coarse, sin_coarse = jnp.cos(coarse), jnp.sin(coarse)
    first = jnp.where(real, cos_fine, -sin_fine)
    second = jnp.where(real, -sin_fine, -cos_fine)
    per = FORM // 128

    def step(i, _):
        shift = (128 - i * per) % 128
        cos_here = pltpu.roll(cos_coarse, shift, 1)
        sin_here = pltpu.roll(sin_coarse, shift, 1)
        for j in range(per):
            at = pl.ds(pl.multiple_of(i * FORM + j * 128, 128), 128)
            cos_b = jnp.broadcast_to(cos_here[:, j : j + 1], shape)
            sin_b = jnp.broadcast_to(sin_here[:, j : j + 1], shape)
            twiddle = (first * cos_b + second * sin_b).astype(BF16).astype(F32)
            for m in range(TAPS):
                weights[pl.ds(m * 32, 32), at] = (
                    taps_ref[pl.ds(m, 1), at] * twiddle
                ).astype(BF16)
        return _

    lax.fori_loop(0, NFFT // FORM, step, 0)


def channelize(volts, weights, acc):
    for n in range(0, NFFT, WIDTH):
        part = lax.dot_general(
            volts[:, :, pl.ds(n, WIDTH)].reshape(FRAMES * 16, WIDTH),
            weights[:, pl.ds(n, WIDTH)],
            (((1,), (1,)), ((), ())),
            preferred_element_type=F32,
        )
        if n == 0:
            acc[...] = part
        else:
            acc[...] += part


def pieces_of(acc, pairs, pieces):
    lane = iota((16, 128), 1)
    group = lane >> 2
    sums = [
        acc[pl.ds(f * 16, 16), :128] + acc[pl.ds((f + 4) * 16, 16), 128:]
        for f in range(SPEC + 3)
    ]
    spectra = []
    for t in range(SPEC):
        x = sums[t + 3]
        for j in (2, 1, 0):
            x = jnp.where(lane < 32 * (j + 1), sums[t + j], x)
        x = x + pltpu.roll(x, 64, 1)
        spectra.append(x + pltpu.roll(x, 32, 1))
    turned = []
    for s in range(8):
        x = spectra[s]
        for q in range(1, 16):
            x = jnp.where((group & 15) == q, spectra[(q + s) % 16], x)
        turned.append(pltpu.roll(x, 4 * s, 1) if s else x)
    for g in range(8):
        x = turned[0]
        for s in range(1, 8):
            x = jnp.where(((group - g) & 7) == s, turned[s], x)
        pairs[g] = x
    low = iota((8, 128), 1) < 64
    for g in range(8):
        even = pairs[g, pl.ds(0, 8, stride=2), :]
        odd = pairs[g, pl.ds(1, 8, stride=2), :]
        pieces[g] = jnp.where(low, even, odd)


def form_onehot(order_ref, onehot):
    lane = iota((128, 128), 1)

    def step(r, _):
        slots = order_ref[pl.ds(r, 1), :].astype(F32)
        wide = jnp.broadcast_to(slots, (128, 128)).T.astype(I32)
        at = pl.ds(pl.multiple_of(r // 8 * 128, 128), 128)
        for j in range(16):
            onehot[r % 8, at, pl.ds(j * 128, 128)] = jnp.where(
                wide == lane + j * 128, 1.0, 0.0
            ).astype(BF16)
        return _

    lax.fori_loop(0, 16, step, 0)


def permute_level(buf, onehot, permuted, z, first):
    slots = jnp.concatenate(
        [buf[y, z].reshape(128, 128).astype(BF16) for y in range(2)], axis=0
    )
    part = lax.dot_general(
        slots, onehot[z], (((0,), (0,)), ((), ())), preferred_element_type=F32
    )
    if first:
        permuted[...] = part
    else:
        permuted[...] += part


def weave_columns(permuted, cols, cols_hbm, out_sem):
    row, col = iota((256, 256), 0), iota((256, 256), 1)
    weave = jnp.where((col >> 1) + (col & 1) * 128 == row, 1.0, 0.0).astype(BF16)
    for j in range(16):
        at = pl.ds(j * 128, 128)
        both = jnp.concatenate([permuted[:64, at], permuted[64:, at]], axis=1)
        cols[:, pl.ds(j * 256, 256)] = jnp.dot(
            both.astype(BF16), weave, preferred_element_type=F32
        ).astype(BF16)
        if j % 4 == 3:
            part = pl.ds((j - 3) * 256, 1024)
            pltpu.make_async_copy(cols.at[:, part], cols_hbm.at[:, part], out_sem).start()


def left_rows(mine, rows, lhs):
    mine = mine * jnp.float32(1.0 / SPEC)
    even = (iota((64, 128), 1) & 1) == 0
    crossed = jnp.where(even, pltpu.roll(mine, 127, 1), -pltpu.roll(mine, 1, 1))
    for o, part in enumerate((mine, crossed)):
        rows[pl.ds(o, 64, stride=4), :] = part
        rows[pl.ds(2 + o, 64, stride=4), :] = pltpu.roll(part, 64, 1)
    both = rows[...]
    channel = (iota(both.shape, 1) >> 1) & 1
    for c in range(2):
        lhs[pl.ds(c * 256, 256), :] = jnp.where(channel == c, both, 0.0).astype(BF16)[:, :64]


def hops(n, size):
    return min(n % size, -n % size)


def spectra_kernel(
    index_hbm, taps_hbm, order_hbm, volts_hbm, lhs_hbm, cols_hbm,
    index_ref, taps_ref, order_ref, volts, weights, acc, pairs, pieces, buf,
    onehot, permuted, rows, lhs, cols, in_sem, volts_sem, lhs_sem, cols_sem,
    s_send, s_recv, r_send, r_recv, y_send, y_recv, c_send, c_recv,
):
    grp, blk = lax.axis_index("grp"), lax.axis_index("blk")
    yh, x = grp // 4, grp % 4
    yl, z, core = blk // 16, (blk // 2) % 8, blk % 2

    inputs = [
        pltpu.make_async_copy(a, b, in_sem.at[n])
        for n, (a, b) in enumerate(
            [(index_hbm, index_ref), (taps_hbm, taps_ref), (order_hbm, order_ref)]
        )
    ]
    for copy in inputs:
        copy.start()
    for f in range(FRAMES):
        pltpu.make_async_copy(
            volts_hbm.at[:, pl.ds(f * NFFT, NFFT)], volts.at[f], volts_sem
        ).start()

    def device(i, j, d):
        return ((yh + i) % 2 * 4 + (x + j) % 4, (yl * 8 + (z + d + 8) % 8) * 2 + core)

    y_device = (grp, ((1 - yl) * 8 + z) * 2 + core)
    c_device = (grp, blk + 1 - 2 * core)
    direct = [
        (i, j, d) for i in range(2) for j in range(4) for d in (0, 1, 7, 2, 6)
        if (i, j, d) != (0, 0, 0)
    ]
    direct.sort(key=lambda m: (-hops(m[2], 8), -2 * m[0] - hops(m[1], 4)))

    barrier = pltpu.get_barrier_semaphore()
    partners = [device(*m) for m in direct] + [y_device, c_device]
    for to in partners:
        pl.semaphore_signal(barrier, inc=1, device_id=to, device_id_type=MESH)

    for copy in inputs:
        copy.wait()
    form_weights(index_ref, taps_ref, weights)
    pltpu.make_async_copy(volts, volts, volts_sem).wait()
    channelize(volts, weights, acc)
    pieces_of(acc, pairs, pieces)
    pl.semaphore_wait(barrier, len(partners))

    sent = []

    def send(ref, s, r, to, src=None):
        pltpu.make_async_remote_copy(
            src_ref=ref if src is None else src, dst_ref=ref, send_sem=s, recv_sem=r,
            device_id=to, device_id_type=MESH,
        ).start()
        if src is None:
            sent.append((ref, s))

    def wait(ref, sem):
        pltpu.make_async_copy(ref, ref, sem).wait()

    def level(y, d, c):
        return buf.at[y, (z - d + 8) % 8, c]

    own = buf.at[yl, z, core, grp]
    for m in direct:
        to = device(*m)
        send(own, s_send, s_recv.at[m[2]], to, src=pieces.at[to[0]])
    buf[yl, z, core, grp] = pieces[grp]
    form_onehot(order_ref, onehot)

    def forward(d):
        here = level(yl, d, core)
        send(here, y_send.at[d], y_recv.at[d], y_device)
        send(here, c_send.at[d], c_recv.at[d], c_device)

    def from_y(d):
        here = level(1 - yl, d, core)
        wait(here, y_recv.at[d])
        send(here, c_send.at[8 + d], c_recv.at[8 + d], c_device)

    done = []

    def permute(d):
        wait(level(yl, d, 1 - core), c_recv.at[d])
        wait(level(1 - yl, d, 1 - core), c_recv.at[8 + d])
        permute_level(buf, onehot, permuted, (z - d + 8) % 8, not done)
        done.append(d)

    half = [pl.ds(0, 4), pl.ds(4, 4)]
    far = (z + 4) % 8
    wait(level(yl, 1, core), s_recv.at[1])
    send(level(yl, 1, core), r_send.at[0], r_recv.at[0], device(0, 0, 2))
    wait(level(yl, 7, core), s_recv.at[7])
    send(level(yl, 7, core), r_send.at[1], r_recv.at[1], device(0, 0, 6))
    wait(level(yl, 2, core), s_recv.at[2])
    send(buf.at[yl, (z + 6) % 8, core, half[0]], r_send.at[2], r_recv.at[2], device(0, 0, 2))
    wait(level(yl, 6, core), s_recv.at[6])
    send(buf.at[yl, (z + 2) % 8, core, half[1]], r_send.at[3], r_recv.at[3], device(0, 0, 6))
    wait(buf.at[yl, z, core, pl.ds(0, 7)], s_recv.at[0])
    for d in (0, 1, 7, 2, 6):
        forward(d)
    for d in (0, 1, 7):
        from_y(d)
    wait(level(yl, 3, core), r_recv.at[0])
    forward(3)
    wait(level(yl, 5, core), r_recv.at[1])
    forward(5)
    from_y(2)
    for h in range(2):
        wait(buf.at[yl, far, core, half[h]], r_recv.at[2 + h])
    forward(4)
    from_y(6)
    permute(0)
    permute(1)
    from_y(3)
    permute(7)
    from_y(5)
    permute(2)
    from_y(4)
    for d in (6, 3, 5):
        permute(d)
    left_rows(buf[pl.ds(yl, 1), pl.ds(z, 1), pl.ds(core, 1)].reshape(64, 128), rows, lhs)
    pltpu.make_async_copy(lhs, lhs_hbm, lhs_sem).start()
    permute(4)
    weave_columns(permuted, cols, cols_hbm, cols_sem)
    for ref, s in sent:
        wait(ref, s)
    for n in range(len(direct) // 8):
        wait(buf.at[0, 0, 0], s_send)
    wait(buf.at[0, 0, 0, pl.ds(0, len(direct) % 8)], s_send)
    wait(lhs, lhs_sem)
    wait(cols, cols_sem)


def spectra_of_all(index, taps, order, volts):
    dma = pltpu.SemaphoreType.DMA
    vmem = pltpu.VMEM
    return pl.pallas_call(
        spectra_kernel,
        out_shape=[
            jax.ShapeDtypeStruct((512, 64), BF16),
            jax.ShapeDtypeStruct((64, 4096), BF16),
        ],
        in_specs=[pl.BlockSpec(memory_space=pltpu.HBM)] * 4,
        out_specs=[pl.BlockSpec(memory_space=pltpu.HBM)] * 2,
        scratch_shapes=[
            pltpu.SMEM((16,), I32),
            vmem((TAPS, NFFT), F32),
            vmem((16, 128), I32),
            vmem((FRAMES, 16, NFFT), BF16),
            vmem((TAPS * 32, NFFT), BF16),
            vmem((FRAMES * 16, TAPS * 32), F32),
            vmem((8, 16, 128), F32),
            vmem((8, 8, 128), F32),
            vmem((2, 8, 2, 8, 8, 128), F32),
            vmem((8, 256, 2048), BF16),
            vmem((128, 2048), F32),
            vmem((256, 128), F32),
            vmem((512, 64), BF16),
            vmem((64, 4096), BF16),
            dma((3,)), dma, dma, dma,
            dma, dma((8,)), dma((4,)), dma((4,)),
            dma((8,)), dma((8,)), dma((16,)), dma((16,)),
        ],
        compiler_params=pltpu.CompilerParams(
            collective_id=0, has_side_effects=True, vmem_limit_bytes=63 << 20
        ),
    )(index, taps, order, volts)


def correlate_kernel(lhs_ref, cols_ref, out_ref):
    x = jnp.dot(lhs_ref[...], cols_ref[...], preferred_element_type=F32)
    out_ref[...] = x.astype(BF16).reshape(2, 128, 2, QBLOCK)


def correlate(lhs, cols):
    return pl.pallas_call(
        correlate_kernel,
        grid=(4096 // QBLOCK,),
        out_shape=jax.ShapeDtypeStruct((2, 128, 2, 4096), BF16),
        in_specs=[
            pl.BlockSpec((512, 64), lambda i: (0, 0)),
            pl.BlockSpec((64, QBLOCK), lambda i: (0, i)),
        ],
        out_specs=pl.BlockSpec((2, 128, 2, QBLOCK), lambda i: (0, 0, 0, i)),
        compiler_params=pltpu.CompilerParams(vmem_limit_bytes=63 << 20),
    )(lhs, cols)


def per_device(voltages, filter_taps, channel_index, antenna_slot_order):
    lhs, cols = spectra_of_all(
        channel_index, filter_taps, antenna_slot_order.reshape(16, 128), voltages
    )
    return correlate(lhs, cols)


def solution(mesh):
    in_specs = (P(("blk", "grp"), None), P(), P(), P())
    out_specs = P("grp", "blk", None, None)
    return jax.shard_map(
        per_device, mesh=mesh, in_specs=in_specs, out_specs=out_specs, check_vma=False
    )
```

```python
import functools
import math

import jax
import jax.numpy as jnp
from jax import lax
from jax.experimental import pallas as pl
from jax.experimental.pallas import tpu as pltpu
from jax.sharding import PartitionSpec as P

F32, BF16, I32 = jnp.float32, jnp.bfloat16, jnp.int32
MESH = pl.DeviceIdType.MESH
NFFT, TAPS, SPEC, FRAMES = 8192, 8, 16, 23
WIDTH = 2048
FORM = 1024
QBLOCK = 1024
PLACE = {0: 0, 1: 1, 7: 2, 2: 3, 6: 4, 3: 5, 5: 6, 4: 7}


def iota(shape, dim):
    return lax.broadcasted_iota(I32, shape, dim)


def form_weights(index_ref, taps_ref, weights):
    shape = (32, 128)
    row, lane = iota(shape, 0), iota(shape, 1)
    channel = jnp.zeros(shape, I32)
    for c in range(16):
        channel = jnp.where(row >> 1 == c, index_ref[c], channel)
    real = (row & 1) == 0
    unit = jnp.float32(2.0 * math.pi / NFFT)
    fine = ((lane * channel) & (NFFT - 1)).astype(F32) * unit
    coarse = (((lane * channel) & 63) * 128).astype(F32) * unit
    cos_fine, sin_fine = jnp.cos(fine), jnp.sin(fine)
    cos_coarse, sin_coarse = jnp.cos(coarse), jnp.sin(coarse)
    first = jnp.where(real, cos_fine, -sin_fine)
    second = jnp.where(real, -sin_fine, -cos_fine)
    per = FORM // 128

    def step(i, _):
        shift = (128 - i * per) % 128
        cos_here = pltpu.roll(cos_coarse, shift, 1)
        sin_here = pltpu.roll(sin_coarse, shift, 1)
        for j in range(per):
            at = pl.ds(pl.multiple_of(i * FORM + j * 128, 128), 128)
            cos_b = jnp.broadcast_to(cos_here[:, j : j + 1], shape)
            sin_b = jnp.broadcast_to(sin_here[:, j : j + 1], shape)
            twiddle = (first * cos_b + second * sin_b).astype(BF16).astype(F32)
            for m in range(TAPS):
                weights[pl.ds(m * 32, 32), at] = (
                    taps_ref[pl.ds(m, 1), at] * twiddle
                ).astype(BF16)
        return _

    lax.fori_loop(0, NFFT // FORM, step, 0)


def channelize(volts, weights, acc):
    for n in range(0, NFFT, WIDTH):
        part = lax.dot_general(
            volts[:, :, pl.ds(n, WIDTH)].reshape(FRAMES * 16, WIDTH),
            weights[:, pl.ds(n, WIDTH)],
            (((1,), (1,)), ((), ())),
            preferred_element_type=F32,
        )
        if n == 0:
            acc[...] = part
        else:
            acc[...] += part


def pieces_of(acc, pairs, pieces):
    lane = iota((16, 128), 1)
    group = lane >> 2
    sums = [
        acc[pl.ds(f * 16, 16), :128] + acc[pl.ds((f + 4) * 16, 16), 128:]
        for f in range(SPEC + 3)
    ]
    spectra = []
    for t in range(SPEC):
        x = sums[t + 3]
        for j in (2, 1, 0):
            x = jnp.where(lane < 32 * (j + 1), sums[t + j], x)
        x = x + pltpu.roll(x, 64, 1)
        spectra.append(x + pltpu.roll(x, 32, 1))
    turned = []
    for s in range(8):
        x = spectra[s]
        for q in range(1, 16):
            x = jnp.where((group & 15) == q, spectra[(q + s) % 16], x)
        turned.append(pltpu.roll(x, 4 * s, 1) if s else x)
    for g in range(8):
        x = turned[0]
        for s in range(1, 8):
            x = jnp.where(((group - g) & 7) == s, turned[s], x)
        pairs[g] = x
    low = iota((8, 128), 1) < 64
    for g in range(8):
        even = pairs[g, pl.ds(0, 8, stride=2), :]
        odd = pairs[g, pl.ds(1, 8, stride=2), :]
        pieces[g] = jnp.where(low, even, odd)


def form_onehot(order_ref, onehot):
    lane = iota((128, 128), 1)

    def step(r, _):
        slots = order_ref[pl.ds(r, 1), :].astype(F32)
        wide = jnp.broadcast_to(slots, (128, 128)).T.astype(I32)
        at = pl.ds(pl.multiple_of(r // 8 * 128, 128), 128)
        for j in range(16):
            onehot[r % 8, at, pl.ds(j * 128, 128)] = jnp.where(
                wide == lane + j * 128, 1.0, 0.0
            ).astype(BF16)
        return _

    lax.fori_loop(0, 16, step, 0)


def permute_level(buf, place, onehot, permuted, z, first):
    slots = jnp.concatenate(
        [buf[y, c, place].reshape(64, 128).astype(BF16) for y in range(2) for c in range(2)],
        axis=0,
    )
    part = lax.dot_general(
        slots, onehot[z], (((0,), (0,)), ((), ())), preferred_element_type=F32
    )
    if first:
        permuted[...] = part
    else:
        permuted[...] += part


def weave_columns(permuted, cols, cols_hbm, out_sem):
    row, col = iota((256, 256), 0), iota((256, 256), 1)
    weave = jnp.where((col >> 1) + (col & 1) * 128 == row, 1.0, 0.0).astype(BF16)
    for j in range(16):
        at = pl.ds(j * 128, 128)
        both = jnp.concatenate([permuted[:64, at], permuted[64:, at]], axis=1)
        cols[:, pl.ds(j * 256, 256)] = jnp.dot(
            both.astype(BF16), weave, preferred_element_type=F32
        ).astype(BF16)
        if j % 4 == 3:
            part = pl.ds((j - 3) * 256, 1024)
            pltpu.make_async_copy(cols.at[:, part], cols_hbm.at[:, part], out_sem).start()


def left_rows(mine, rows, lhs):
    mine = mine * jnp.float32(1.0 / SPEC)
    even = (iota((64, 128), 1) & 1) == 0
    crossed = jnp.where(even, pltpu.roll(mine, 127, 1), -pltpu.roll(mine, 1, 1))
    for o, part in enumerate((mine, crossed)):
        rows[pl.ds(o, 64, stride=4), :] = part
        rows[pl.ds(2 + o, 64, stride=4), :] = pltpu.roll(part, 64, 1)
    both = rows[...]
    channel = (iota(both.shape, 1) >> 1) & 1
    for c in range(2):
        lhs[pl.ds(c * 256, 256), :] = jnp.where(channel == c, both, 0.0).astype(BF16)[:, :64]


def hops(n, size):
    return min(n % size, -n % size)


def spectra_kernel(
    index_hbm, taps_hbm, order_hbm, volts_hbm, lhs_hbm, cols_hbm,
    index_ref, taps_ref, order_ref, volts, weights, acc, pairs, pieces, buf,
    onehot, permuted, rows, lhs, cols, in_sem, volts_sem, lhs_sem, cols_sem,
    s_send, s_recv, t_recv, r_send, r_recv, y_send, y_recv, c_send, c_recv,
):
    grp, blk = lax.axis_index("grp"), lax.axis_index("blk")
    yh, x = grp // 4, lax.rem(grp, 4)
    yl, z, core = blk // 16, lax.rem(blk // 2, 8), lax.rem(blk, 2)

    inputs = [
        pltpu.make_async_copy(a, b, in_sem.at[n])
        for n, (a, b) in enumerate(
            [(index_hbm, index_ref), (taps_hbm, taps_ref), (order_hbm, order_ref)]
        )
    ]
    for copy in inputs:
        copy.start()
    for f in range(FRAMES):
        pltpu.make_async_copy(
            volts_hbm.at[:, pl.ds(f * NFFT, NFFT)], volts.at[f], volts_sem
        ).start()

    def device(i, j, d, f=0):
        return (
            lax.rem(yh + i, 2) * 4 + lax.rem(x + j, 4),
            (lax.rem(yl + f, 2) * 8 + lax.rem(z + d, 8)) * 2 + core,
        )

    c_device = (grp, blk + 1 - 2 * core)
    near = (0, 1, 7)
    direct = [(i, j, d, 0) for i in range(2) for j in range(4) for d in near + (2, 6)]
    direct += [(i, j, d, 1) for i in range(2) for j in range(4) for d in near]
    direct.remove((0, 0, 0, 0))
    direct.sort(key=lambda m: (m[3], -hops(m[2], 8), -2 * m[0] - hops(m[1], 4)))

    barrier = pltpu.get_barrier_semaphore()
    partners = [device(*m) for m in direct] + [c_device]
    for to in partners:
        pl.semaphore_signal(barrier, inc=1, device_id=to, device_id_type=MESH)

    for copy in inputs:
        copy.wait()
    form_weights(index_ref, taps_ref, weights)
    pltpu.make_async_copy(volts, volts, volts_sem).wait()
    channelize(volts, weights, acc)
    pieces_of(acc, pairs, pieces)
    pl.semaphore_wait(barrier, len(partners))

    sent = []

    def send(src, s, r, to, dst=None):
        dst = src if dst is None else dst
        pltpu.make_async_remote_copy(
            src_ref=src, dst_ref=dst, send_sem=s, recv_sem=r,
            device_id=to, device_id_type=MESH,
        ).start()
        sent.append((src, s))

    def wait(ref, sem):
        pltpu.make_async_copy(ref, ref, sem).wait()

    def held(y, first, count=1):
        return buf.at[y, core, pl.ds(first, count)]

    for m in direct:
        to = device(*m)
        pltpu.make_async_remote_copy(
            src_ref=pieces.at[to[0]], dst_ref=buf.at[yl, core, PLACE[m[2]], grp],
            send_sem=s_send, recv_sem=(t_recv if m[3] else s_recv).at[m[2]],
            device_id=to, device_id_type=MESH,
        ).start()
    buf[yl, core, 0, grp] = pieces[grp]
    form_onehot(order_ref, onehot)

    y_device = device(0, 0, 0, 1)
    up, down = device(0, 0, 2), device(0, 0, 6)

    def to_y(n, first, count):
        send(held(yl, first, count), y_send.at[n], y_recv.at[n], y_device)

    def to_core(n, y, first, count):
        send(held(y, first, count), c_send.at[n], c_recv.at[n], c_device)

    def from_core(n, y, first, count):
        wait(buf.at[y, 1 - core, pl.ds(first, count)], c_recv.at[n])

    def permute(d):
        permute_level(buf, PLACE[d], onehot, permuted, lax.rem(z - d + 8, 8), d == 0)

    def half(place, h):
        return buf.at[yl, core, place, pl.ds(4 * h, 4)]

    wait(held(yl, 1), s_recv.at[1])
    send(held(yl, 1), r_send.at[0], r_recv.at[0], up, held(yl, 5))
    wait(held(yl, 2), s_recv.at[7])
    send(held(yl, 2), r_send.at[1], r_recv.at[1], down, held(yl, 6))
    wait(held(yl, 3), s_recv.at[2])
    send(half(3, 0), r_send.at[2], r_recv.at[2], up, half(7, 0))
    wait(held(yl, 4), s_recv.at[6])
    send(half(4, 1), r_send.at[3], r_recv.at[3], down, half(7, 1))
    to_y(0, 3, 2)
    wait(buf.at[yl, core, 0, pl.ds(0, 7)], s_recv.at[0])
    to_core(0, yl, 0, 5)
    for d in near:
        wait(held(1 - yl, PLACE[d]), t_recv.at[d])
    to_core(1, 1 - yl, 0, 3)
    wait(held(yl, 5), r_recv.at[0])
    wait(held(yl, 6), r_recv.at[1])
    to_y(1, 5, 2)
    to_core(2, yl, 5, 2)
    wait(held(1 - yl, 3, 2), y_recv.at[0])
    to_core(3, 1 - yl, 3, 2)
    for h in range(2):
        wait(half(7, h), r_recv.at[2 + h])
    to_y(2, 7, 1)
    to_core(4, yl, 7, 1)
    from_core(0, yl, 0, 5)
    from_core(1, 1 - yl, 0, 3)
    for d in near:
        permute(d)
    wait(held(1 - yl, 5, 2), y_recv.at[1])
    to_core(5, 1 - yl, 5, 2)
    from_core(3, 1 - yl, 3, 2)
    permute(2)
    permute(6)
    wait(held(1 - yl, 7), y_recv.at[2])
    to_core(6, 1 - yl, 7, 1)
    from_core(2, yl, 5, 2)
    from_core(5, 1 - yl, 5, 2)
    permute(3)
    permute(5)
    left_rows(buf[pl.ds(yl, 1), pl.ds(core, 1), pl.ds(0, 1)].reshape(64, 128), rows, lhs)
    pltpu.make_async_copy(lhs, lhs_hbm, lhs_sem).start()
    from_core(4, yl, 7, 1)
    from_core(6, 1 - yl, 7, 1)
    permute(4)
    weave_columns(permuted, cols, cols_hbm, cols_sem)
    for ref, s in sent:
        wait(ref, s)
    for n in range(len(direct) // 8):
        wait(buf.at[0, 0, 0], s_send)
    wait(buf.at[0, 0, 0, pl.ds(0, len(direct) % 8)], s_send)
    wait(lhs, lhs_sem)
    wait(cols, cols_sem)


def spectra_of_all(index, taps, order, volts):
    dma = pltpu.SemaphoreType.DMA
    vmem = pltpu.VMEM
    return pl.pallas_call(
        spectra_kernel,
        out_shape=[
            jax.ShapeDtypeStruct((512, 64), BF16),
            jax.ShapeDtypeStruct((64, 4096), BF16),
        ],
        in_specs=[pl.BlockSpec(memory_space=pltpu.HBM)] * 4,
        out_specs=[pl.BlockSpec(memory_space=pltpu.HBM)] * 2,
        scratch_shapes=[
            pltpu.SMEM((16,), I32),
            vmem((TAPS, NFFT), F32),
            vmem((16, 128), I32),
            vmem((FRAMES, 16, NFFT), BF16),
            vmem((TAPS * 32, NFFT), BF16),
            vmem((FRAMES * 16, TAPS * 32), F32),
            vmem((8, 16, 128), F32),
            vmem((8, 8, 128), F32),
            vmem((2, 2, 8, 8, 8, 128), F32),
            vmem((8, 256, 2048), BF16),
            vmem((128, 2048), F32),
            vmem((256, 128), F32),
            vmem((512, 64), BF16),
            vmem((64, 4096), BF16),
            dma((3,)), dma, dma, dma,
            dma, dma((8,)), dma((8,)), dma((4,)), dma((4,)),
            dma((3,)), dma((3,)), dma((7,)), dma((7,)),
        ],
        compiler_params=pltpu.CompilerParams(
            collective_id=0, has_side_effects=True, vmem_limit_bytes=63 << 20
        ),
    )(index, taps, order, volts)


def correlate_kernel(lhs_hbm, cols_hbm, out_hbm, lhs, cols, out, lhs_sem, cols_sem, out_sem):
    steps = 4096 // QBLOCK
    left = pltpu.make_async_copy(lhs_hbm, lhs, lhs_sem)
    left.start()
    right = []
    for i in range(steps):
        at = pl.ds(i * QBLOCK, QBLOCK)
        right.append(pltpu.make_async_copy(cols_hbm.at[:, at], cols.at[:, at], cols_sem.at[i]))
        right[i].start()
    left.wait()
    for i in range(steps):
        at = pl.ds(i * QBLOCK, QBLOCK)
        right[i].wait()
        for c in range(2):
            x = jnp.dot(lhs[pl.ds(c * 256, 256), :], cols[:, at], preferred_element_type=F32)
            out[i, c] = x.astype(BF16).reshape(128, 2, QBLOCK)
        pltpu.make_async_copy(out.at[i], out_hbm.at[:, :, :, at], out_sem).start()
    pltpu.make_async_copy(out, out, out_sem).wait()


def correlate(lhs, cols):
    dma = pltpu.SemaphoreType.DMA
    vmem = pltpu.VMEM
    return pl.pallas_call(
        correlate_kernel,
        out_shape=jax.ShapeDtypeStruct((2, 128, 2, 4096), BF16),
        in_specs=[pl.BlockSpec(memory_space=pltpu.HBM)] * 2,
        out_specs=pl.BlockSpec(memory_space=pltpu.HBM),
        scratch_shapes=[
            vmem((512, 64), BF16),
            vmem((64, 4096), BF16),
            vmem((4096 // QBLOCK, 2, 128, 2, QBLOCK), BF16),
            dma, dma((4096 // QBLOCK,)), dma,
        ],
        compiler_params=pltpu.CompilerParams(vmem_limit_bytes=63 << 20),
    )(lhs, cols)


def per_device(voltages, filter_taps, channel_index, antenna_slot_order):
    lhs, cols = spectra_of_all(
        channel_index, filter_taps, antenna_slot_order.reshape(16, 128), voltages
    )
    return correlate(lhs, cols)


def solution(mesh):
    in_specs = (P(("blk", "grp"), None), P(), P(), P())
    out_specs = P("grp", "blk", None, None)
    return jax.shard_map(
        per_device, mesh=mesh, in_specs=in_specs, out_specs=out_specs, check_vma=False
    )
```

```python
import functools
import math

import jax
import jax.numpy as jnp
from jax import lax
from jax.experimental import pallas as pl
from jax.experimental.pallas import tpu as pltpu
from jax.sharding import PartitionSpec as P

F32, BF16, I32 = jnp.float32, jnp.bfloat16, jnp.int32
MESH = pl.DeviceIdType.MESH
NFFT, TAPS, SPEC, FRAMES = 8192, 8, 16, 23
GROUPS = ((0, 12), (12, 11))
FORM = 1024
QBLOCK = 1024
PLACE = {0: 0, 1: 1, 7: 2, 2: 3, 6: 4, 3: 5, 5: 6, 4: 7}


def iota(shape, dim):
    return lax.broadcasted_iota(I32, shape, dim)


def cos_turns(phase):
    phase = phase & (NFFT - 1)
    fold = jnp.where(phase > NFFT // 2, NFFT - phase, phase)
    x = (NFFT // 4 - fold).astype(F32) * jnp.float32(2.0 * math.pi / NFFT)
    square = x * x
    total = jnp.full(x.shape, 1.0 / math.factorial(13), F32)
    for n in (11, 9, 7, 5, 3, 1):
        total = total * square + jnp.float32((-1) ** (n // 2) / math.factorial(n))
    return total * x


def tables(index_ref):
    shape = (32, 128)
    row, lane = iota(shape, 0), iota(shape, 1)
    channel = jnp.zeros(shape, I32)
    for c in range(16):
        channel = jnp.where(row >> 1 == c, index_ref[c], channel)
    quarter = NFFT // 4
    fine = lane * channel + (row & 1) * quarter
    coarse = (lane & 63) * channel * 128 - (lane >> 6) * quarter
    return cos_turns(fine), cos_turns(fine + quarter), cos_turns(coarse)


def form_weights(factors, taps_ref, weights):
    first, second, coarse = factors
    for block in range(NFFT // 128):
        cos_b = jnp.broadcast_to(coarse[:, block : block + 1], first.shape)
        sin_b = jnp.broadcast_to(coarse[:, 64 + block : 65 + block], first.shape)
        twiddle = (first * cos_b + second * sin_b).astype(BF16).astype(F32)
        at = pl.ds(block * 128 % FORM, 128)
        for m in range(TAPS):
            weights[block * 128 // FORM][pl.ds(m * 32, 32), at] = (
                taps_ref[pl.ds(m, 1), pl.ds(block * 128, 128)] * twiddle
            ).astype(BF16)


def channelize(volts, weights, acc, first, count):
    at = pl.ds(first * 16, count * 16)
    for n, part in enumerate(weights):
        x = lax.dot_general(
            volts[pl.ds(first, count), :, pl.ds(n * FORM, FORM)].reshape(count * 16, FORM),
            part[...],
            (((1,), (1,)), ((), ())),
            preferred_element_type=F32,
        )
        if n == 0:
            acc[at, :] = x
        else:
            acc[at, :] += x


def pieces_of(acc, pairs, pieces):
    lane = iota((16, 128), 1)
    group = lane >> 2
    sums = [
        acc[pl.ds(f * 16, 16), :128] + acc[pl.ds((f + 4) * 16, 16), 128:]
        for f in range(SPEC + 3)
    ]
    spectra = []
    for t in range(SPEC):
        x = sums[t + 3]
        for j in (2, 1, 0):
            x = jnp.where(lane < 32 * (j + 1), sums[t + j], x)
        x = x + pltpu.roll(x, 64, 1)
        spectra.append(x + pltpu.roll(x, 32, 1))
    turned = []
    for s in range(8):
        x = spectra[s]
        for q in range(1, 16):
            x = jnp.where((group & 15) == q, spectra[(q + s) % 16], x)
        turned.append(pltpu.roll(x, 4 * s, 1) if s else x)
    for g in range(8):
        x = turned[0]
        for s in range(1, 8):
            x = jnp.where(((group - g) & 7) == s, turned[s], x)
        pairs[g] = x
    low = iota((8, 128), 1) < 64
    for g in range(8):
        even = pairs[g, pl.ds(0, 8, stride=2), :]
        odd = pairs[g, pl.ds(1, 8, stride=2), :]
        pieces[g] = jnp.where(low, even, odd)


def form_onehot(order_ref, onehot):
    lane = iota((128, 128), 1)

    def step(r, _):
        slots = order_ref[pl.ds(r, 1), :].astype(F32)
        wide = jnp.broadcast_to(slots, (128, 128)).T.astype(I32)
        at = pl.ds(pl.multiple_of(r // 8 * 128, 128), 128)
        for j in range(16):
            onehot[r % 8, at, pl.ds(j * 128, 128)] = jnp.where(
                wide == lane + j * 128, 1.0, 0.0
            ).astype(BF16)
        return _

    lax.fori_loop(0, 16, step, 0)


def permute_level(buf, place, onehot, permuted, z, first):
    slots = jnp.concatenate(
        [buf[y, c, place].reshape(64, 128).astype(BF16) for y in range(2) for c in range(2)],
        axis=0,
    )
    part = lax.dot_general(
        slots, onehot[z], (((0,), (0,)), ((), ())), preferred_element_type=F32
    )
    if first:
        permuted[...] = part
    else:
        permuted[...] += part


def weave_columns(permuted, cols, cols_hbm, out_sem):
    row, col = iota((256, 256), 0), iota((256, 256), 1)
    weave = jnp.where((col >> 1) + (col & 1) * 128 == row, 1.0, 0.0).astype(BF16)
    for j in range(16):
        at = pl.ds(j * 128, 128)
        both = jnp.concatenate([permuted[:64, at], permuted[64:, at]], axis=1)
        cols[:, pl.ds(j * 256, 256)] = jnp.dot(
            both.astype(BF16), weave, preferred_element_type=F32
        ).astype(BF16)
        if j % 4 == 3:
            part = pl.ds((j - 3) * 256, 1024)
            pltpu.make_async_copy(cols.at[:, part], cols_hbm.at[:, part], out_sem).start()


def left_rows(mine, rows, lhs):
    mine = mine * jnp.float32(1.0 / SPEC)
    even = (iota((64, 128), 1) & 1) == 0
    crossed = jnp.where(even, pltpu.roll(mine, 127, 1), -pltpu.roll(mine, 1, 1))
    for o, part in enumerate((mine, crossed)):
        rows[pl.ds(o, 64, stride=4), :] = part
        rows[pl.ds(2 + o, 64, stride=4), :] = pltpu.roll(part, 64, 1)
    both = rows[...]
    channel = (iota(both.shape, 1) >> 1) & 1
    for c in range(2):
        lhs[pl.ds(c * 256, 256), :] = jnp.where(channel == c, both, 0.0).astype(BF16)[:, :64]


def hops(n, size):
    return min(n % size, -n % size)


def spectra_kernel(
    index_hbm, taps_hbm, order_hbm, volts_hbm, lhs_hbm, cols_hbm,
    index_ref, taps_ref, order_ref, volts, acc, pairs, pieces, buf,
    onehot, permuted, rows, lhs, cols, in_sem, volts_sem, lhs_sem, cols_sem,
    s_send, s_recv, t_recv, r_send, r_recv, y_send, y_recv, c_send, c_recv, *weights,
):
    grp, blk = lax.axis_index("grp"), lax.axis_index("blk")
    yh, x = grp // 4, lax.rem(grp, 4)
    yl, z, core = blk // 16, lax.rem(blk // 2, 8), lax.rem(blk, 2)

    inputs = [
        pltpu.make_async_copy(a, b, in_sem.at[n])
        for n, (a, b) in enumerate(
            [(index_hbm, index_ref), (taps_hbm, taps_ref), (order_hbm, order_ref)]
        )
    ]
    for copy in inputs[:2]:
        copy.start()
    for n, (first, count) in enumerate(GROUPS):
        for f in range(first, first + count):
            pltpu.make_async_copy(
                volts_hbm.at[:, pl.ds(f * NFFT, NFFT)], volts.at[f], volts_sem.at[n]
            ).start(priority=f % 2)

    def device(i, j, d, f=0):
        return (
            lax.rem(yh + i, 2) * 4 + lax.rem(x + j, 4),
            (lax.rem(yl + f, 2) * 8 + lax.rem(z + d, 8)) * 2 + core,
        )

    c_device = (grp, blk + 1 - 2 * core)
    near = (0, 1, 7)
    direct = [(i, j, d, 0) for i in range(2) for j in range(4) for d in near + (2, 6)]
    direct += [(i, j, d, 1) for i in range(2) for j in range(4) for d in near]
    direct.remove((0, 0, 0, 0))
    direct.sort(key=lambda m: (m[3], -hops(m[2], 8), -2 * m[0] - hops(m[1], 4)))

    barrier = pltpu.get_barrier_semaphore()
    partners = [device(*m) for m in direct] + [c_device]
    for to in partners:
        pl.semaphore_signal(barrier, inc=1, device_id=to, device_id_type=MESH)

    inputs[2].start()
    inputs[0].wait()
    factors = tables(index_ref)
    inputs[1].wait()
    form_weights(factors, taps_ref, weights)
    for n, (first, count) in enumerate(GROUPS):
        part = volts.at[pl.ds(first, count)]
        pltpu.make_async_copy(part, part, volts_sem.at[n]).wait()
        channelize(volts, weights, acc, first, count)
    pieces_of(acc, pairs, pieces)
    pl.semaphore_wait(barrier, len(partners))

    sent = []

    def send(src, s, r, to, dst=None):
        dst = src if dst is None else dst
        pltpu.make_async_remote_copy(
            src_ref=src, dst_ref=dst, send_sem=s, recv_sem=r,
            device_id=to, device_id_type=MESH,
        ).start()
        sent.append((src, s))

    def wait(ref, sem):
        pltpu.make_async_copy(ref, ref, sem).wait()

    def held(y, first, count=1):
        return buf.at[y, core, pl.ds(first, count)]

    for m in direct:
        to = device(*m)
        pltpu.make_async_remote_copy(
            src_ref=pieces.at[to[0]], dst_ref=buf.at[yl, core, PLACE[m[2]], grp],
            send_sem=s_send, recv_sem=(t_recv if m[3] else s_recv).at[m[2]],
            device_id=to, device_id_type=MESH,
        ).start()
    buf[yl, core, 0, grp] = pieces[grp]
    inputs[2].wait()
    form_onehot(order_ref, onehot)

    y_device = device(0, 0, 0, 1)
    up, down = device(0, 0, 2), device(0, 0, 6)

    def to_y(n, first, count):
        send(held(yl, first, count), y_send.at[n], y_recv.at[n], y_device)

    def to_core(n, y, first, count):
        send(held(y, first, count), c_send.at[n], c_recv.at[n], c_device)

    def from_core(n, y, first, count):
        wait(buf.at[y, 1 - core, pl.ds(first, count)], c_recv.at[n])

    def permute(d):
        permute_level(buf, PLACE[d], onehot, permuted, lax.rem(z - d + 8, 8), d == 0)

    def half(place, h):
        return buf.at[yl, core, place, pl.ds(4 * h, 4)]

    wait(held(yl, 1), s_recv.at[1])
    send(held(yl, 1), r_send.at[0], r_recv.at[0], up, held(yl, 5))
    wait(held(yl, 2), s_recv.at[7])
    send(held(yl, 2), r_send.at[1], r_recv.at[1], down, held(yl, 6))
    wait(held(yl, 3), s_recv.at[2])
    send(half(3, 0), r_send.at[2], r_recv.at[2], up, half(7, 0))
    wait(held(yl, 4), s_recv.at[6])
    send(half(4, 1), r_send.at[3], r_recv.at[3], down, half(7, 1))
    to_y(0, 3, 2)
    wait(buf.at[yl, core, 0, pl.ds(0, 7)], s_recv.at[0])
    to_core(0, yl, 0, 5)
    for d in near:
        wait(held(1 - yl, PLACE[d]), t_recv.at[d])
    to_core(1, 1 - yl, 0, 3)
    wait(held(yl, 5), r_recv.at[0])
    wait(held(yl, 6), r_recv.at[1])
    to_y(1, 5, 2)
    to_core(2, yl, 5, 2)
    wait(held(1 - yl, 3, 2), y_recv.at[0])
    to_core(3, 1 - yl, 3, 2)
    for h in range(2):
        wait(half(7, h), r_recv.at[2 + h])
    to_y(2, 7, 1)
    to_core(4, yl, 7, 1)
    from_core(0, yl, 0, 5)
    from_core(1, 1 - yl, 0, 3)
    for d in near:
        permute(d)
    wait(held(1 - yl, 5, 2), y_recv.at[1])
    to_core(5, 1 - yl, 5, 2)
    from_core(3, 1 - yl, 3, 2)
    permute(2)
    permute(6)
    wait(held(1 - yl, 7), y_recv.at[2])
    to_core(6, 1 - yl, 7, 1)
    from_core(2, yl, 5, 2)
    from_core(5, 1 - yl, 5, 2)
    permute(3)
    permute(5)
    left_rows(buf[pl.ds(yl, 1), pl.ds(core, 1), pl.ds(0, 1)].reshape(64, 128), rows, lhs)
    pltpu.make_async_copy(lhs, lhs_hbm, lhs_sem).start()
    from_core(4, yl, 7, 1)
    from_core(6, 1 - yl, 7, 1)
    permute(4)
    weave_columns(permuted, cols, cols_hbm, cols_sem)
    for ref, s in sent:
        wait(ref, s)
    for n in range(len(direct) // 8):
        wait(buf.at[0, 0, 0], s_send)
    wait(buf.at[0, 0, 0, pl.ds(0, len(direct) % 8)], s_send)
    wait(lhs, lhs_sem)
    wait(cols, cols_sem)


def spectra_of_all(index, taps, order, volts):
    dma = pltpu.SemaphoreType.DMA
    vmem = pltpu.VMEM
    return pl.pallas_call(
        spectra_kernel,
        out_shape=[
            jax.ShapeDtypeStruct((512, 64), BF16),
            jax.ShapeDtypeStruct((64, 4096), BF16),
        ],
        in_specs=[pl.BlockSpec(memory_space=pltpu.HBM)] * 4,
        out_specs=[pl.BlockSpec(memory_space=pltpu.HBM)] * 2,
        scratch_shapes=[
            pltpu.SMEM((16,), I32),
            vmem((TAPS, NFFT), F32),
            vmem((16, 128), I32),
            vmem((FRAMES, 16, NFFT), BF16),
            vmem((FRAMES * 16, TAPS * 32), F32),
            vmem((8, 16, 128), F32),
            vmem((8, 8, 128), F32),
            vmem((2, 2, 8, 8, 8, 128), F32),
            vmem((8, 256, 2048), BF16),
            vmem((128, 2048), F32),
            vmem((256, 128), F32),
            vmem((512, 64), BF16),
            vmem((64, 4096), BF16),
            dma((3,)), dma((len(GROUPS),)), dma, dma,
            dma, dma((8,)), dma((8,)), dma((4,)), dma((4,)),
            dma((3,)), dma((3,)), dma((7,)), dma((7,)),
            *[vmem((TAPS * 32, FORM), BF16)] * (NFFT // FORM),
        ],
        compiler_params=pltpu.CompilerParams(
            collective_id=0, has_side_effects=True, vmem_limit_bytes=63 << 20
        ),
    )(index, taps, order, volts)


def correlate_kernel(lhs_hbm, cols_hbm, out_hbm, lhs, cols, out, lhs_sem, cols_sem, out_sem):
    steps = 4096 // QBLOCK
    left = pltpu.make_async_copy(lhs_hbm, lhs, lhs_sem)
    left.start()
    right = []
    for i in range(steps):
        at = pl.ds(i * QBLOCK, QBLOCK)
        right.append(pltpu.make_async_copy(cols_hbm.at[:, at], cols.at[:, at], cols_sem.at[i]))
        right[i].start()
    left.wait()
    for i in range(steps):
        at = pl.ds(i * QBLOCK, QBLOCK)
        right[i].wait()
        for c in range(2):
            x = jnp.dot(lhs[pl.ds(c * 256, 256), :], cols[:, at], preferred_element_type=F32)
            out[i, c] = x.astype(BF16).reshape(128, 2, QBLOCK)
        pltpu.make_async_copy(out.at[i], out_hbm.at[:, :, :, at], out_sem).start()
    pltpu.make_async_copy(out, out, out_sem).wait()


def correlate(lhs, cols):
    dma = pltpu.SemaphoreType.DMA
    vmem = pltpu.VMEM
    return pl.pallas_call(
        correlate_kernel,
        out_shape=jax.ShapeDtypeStruct((2, 128, 2, 4096), BF16),
        in_specs=[pl.BlockSpec(memory_space=pltpu.HBM)] * 2,
        out_specs=pl.BlockSpec(memory_space=pltpu.HBM),
        scratch_shapes=[
            vmem((512, 64), BF16),
            vmem((64, 4096), BF16),
            vmem((4096 // QBLOCK, 2, 128, 2, QBLOCK), BF16),
            dma, dma((4096 // QBLOCK,)), dma,
        ],
        compiler_params=pltpu.CompilerParams(vmem_limit_bytes=63 << 20),
    )(lhs, cols)


def per_device(voltages, filter_taps, channel_index, antenna_slot_order):
    lhs, cols = spectra_of_all(
        channel_index, filter_taps, antenna_slot_order.reshape(16, 128), voltages
    )
    return correlate(lhs, cols)


def solution(mesh):
    in_specs = (P(("blk", "grp"), None), P(), P(), P())
    out_specs = P("grp", "blk", None, None)
    return jax.shard_map(
        per_device, mesh=mesh, in_specs=in_specs, out_specs=out_specs, check_vma=False
    )
```

```python
import functools
import math

import jax
import jax.numpy as jnp
from jax import lax
from jax.experimental import pallas as pl
from jax.experimental.pallas import tpu as pltpu
from jax.sharding import PartitionSpec as P

F32, BF16, I32 = jnp.float32, jnp.bfloat16, jnp.int32
MESH = pl.DeviceIdType.MESH
NFFT, TAPS, SPEC, FRAMES = 8192, 8, 16, 23
GROUPS = ((0, 12), (12, 11))
FORM = 1024
QBLOCK = 1024
PLACE = {0: 0, 1: 1, 7: 2, 2: 3, 6: 4, 3: 5, 5: 6, 4: 7}


def iota(shape, dim):
    return lax.broadcasted_iota(I32, shape, dim)


def cos_turns(phase):
    phase = phase & (NFFT - 1)
    fold = jnp.where(phase > NFFT // 2, NFFT - phase, phase)
    x = (NFFT // 4 - fold).astype(F32) * jnp.float32(2.0 * math.pi / NFFT)
    square = x * x
    total = jnp.full(x.shape, 1.0 / math.factorial(13), F32)
    for n in (11, 9, 7, 5, 3, 1):
        total = total * square + jnp.float32((-1) ** (n // 2) / math.factorial(n))
    return total * x


def tables(index_ref):
    shape = (32, 128)
    row, lane = iota(shape, 0), iota(shape, 1)
    channel = jnp.zeros(shape, I32)
    for c in range(16):
        channel = jnp.where(row >> 1 == c, index_ref[c], channel)
    quarter = NFFT // 4
    fine = lane * channel + (row & 1) * quarter
    coarse = (lane & 63) * channel * 128 - (lane >> 6) * quarter
    return cos_turns(fine), cos_turns(fine + quarter), cos_turns(coarse)


def form_weights(factors, taps_ref, weights):
    first, second, coarse = factors
    for block in range(NFFT // 128):
        cos_b = jnp.broadcast_to(coarse[:, block : block + 1], first.shape)
        sin_b = jnp.broadcast_to(coarse[:, 64 + block : 65 + block], first.shape)
        twiddle = (first * cos_b + second * sin_b).astype(BF16).astype(F32)
        at = pl.ds(block * 128 % FORM, 128)
        for m in range(TAPS):
            weights[block * 128 // FORM][pl.ds(m * 32, 32), at] = (
                taps_ref[pl.ds(m, 1), pl.ds(block * 128, 128)] * twiddle
            ).astype(BF16)


def channelize(volts, weights, acc, first, count):
    at = pl.ds(first * 16, count * 16)
    for n, part in enumerate(weights):
        x = lax.dot_general(
            volts[pl.ds(first, count), :, pl.ds(n * FORM, FORM)].reshape(count * 16, FORM),
            part[...],
            (((1,), (1,)), ((), ())),
            preferred_element_type=F32,
        )
        if n == 0:
            acc[at, :] = x
        else:
            acc[at, :] += x


def pieces_of(acc, pairs, pieces):
    lane = iota((16, 128), 1)
    group = lane >> 2
    sums = [
        acc[pl.ds(f * 16, 16), :128] + acc[pl.ds((f + 4) * 16, 16), 128:]
        for f in range(SPEC + 3)
    ]
    spectra = []
    for t in range(SPEC):
        x = sums[t + 3]
        for j in (2, 1, 0):
            x = jnp.where(lane < 32 * (j + 1), sums[t + j], x)
        x = x + pltpu.roll(x, 64, 1)
        spectra.append(x + pltpu.roll(x, 32, 1))
    turned = []
    for s in range(8):
        x = spectra[s]
        for q in range(1, 16):
            x = jnp.where((group & 15) == q, spectra[(q + s) % 16], x)
        turned.append(pltpu.roll(x, 4 * s, 1) if s else x)
    for g in range(8):
        x = turned[0]
        for s in range(1, 8):
            x = jnp.where(((group - g) & 7) == s, turned[s], x)
        pairs[g] = x
    low = iota((8, 128), 1) < 64
    for g in range(8):
        even = pairs[g, pl.ds(0, 8, stride=2), :]
        odd = pairs[g, pl.ds(1, 8, stride=2), :]
        pieces[g] = jnp.where(low, even, odd)


def form_onehot(order_ref, onehot):
    lane = iota((128, 128), 1)

    def step(r, _):
        slots = order_ref[pl.ds(r, 1), :].astype(F32)
        wide = jnp.broadcast_to(slots, (128, 128)).T.astype(I32)
        at = pl.ds(pl.multiple_of(r // 8 * 128, 128), 128)
        for j in range(16):
            onehot[r % 8, at, pl.ds(j * 128, 128)] = jnp.where(
                wide == lane + j * 128, 1.0, 0.0
            ).astype(BF16)
        return _

    lax.fori_loop(0, 16, step, 0)


def permute_level(buf, place, onehot, permuted, z, first):
    slots = jnp.concatenate(
        [buf[y, c, place].reshape(64, 128).astype(BF16) for y in range(2) for c in range(2)],
        axis=0,
    )
    part = lax.dot_general(
        slots, onehot[z], (((0,), (0,)), ((), ())), preferred_element_type=F32
    )
    if first:
        permuted[...] = part
    else:
        permuted[...] += part


def weave_columns(permuted, cols, cols_hbm, out_sem):
    row, col = iota((256, 256), 0), iota((256, 256), 1)
    weave = jnp.where((col >> 1) + (col & 1) * 128 == row, 1.0, 0.0).astype(BF16)
    for j in range(16):
        at = pl.ds(j * 128, 128)
        both = jnp.concatenate([permuted[:64, at], permuted[64:, at]], axis=1)
        cols[:, pl.ds(j * 256, 256)] = jnp.dot(
            both.astype(BF16), weave, preferred_element_type=F32
        ).astype(BF16)
        if j % 4 == 3:
            part = pl.ds((j - 3) * 256, 1024)
            pltpu.make_async_copy(cols.at[:, part], cols_hbm.at[:, part], out_sem).start()


def left_rows(mine, rows, lhs):
    mine = mine * jnp.float32(1.0 / SPEC)
    even = (iota((64, 128), 1) & 1) == 0
    crossed = jnp.where(even, pltpu.roll(mine, 127, 1), -pltpu.roll(mine, 1, 1))
    for o, part in enumerate((mine, crossed)):
        rows[pl.ds(o, 64, stride=4), :] = part
        rows[pl.ds(2 + o, 64, stride=4), :] = pltpu.roll(part, 64, 1)
    both = rows[...]
    channel = (iota(both.shape, 1) >> 1) & 1
    for c in range(2):
        lhs[pl.ds(c * 256, 256), :] = jnp.where(channel == c, both, 0.0).astype(BF16)[:, :64]


def hops(n, size):
    return min(n % size, -n % size)


def spectra_kernel(
    index_hbm, taps_hbm, order_hbm, volts_hbm, lhs_hbm, cols_hbm,
    index_ref, taps_ref, order_ref, volts, acc, pairs, pieces, buf,
    onehot, permuted, rows, lhs, cols, in_sem, volts_sem, lhs_sem, cols_sem,
    s_send, s_recv, t_recv, r_send, r_recv, y_send, y_recv, c_send, c_recv, *weights,
):
    grp, blk = lax.axis_index("grp"), lax.axis_index("blk")
    yh, x = grp // 4, lax.rem(grp, 4)
    yl, z, core = blk // 16, lax.rem(blk // 2, 8), lax.rem(blk, 2)

    inputs = [
        pltpu.make_async_copy(a, b, in_sem.at[n])
        for n, (a, b) in enumerate(
            [(index_hbm, index_ref), (taps_hbm, taps_ref), (order_hbm, order_ref)]
        )
    ]
    for copy in inputs[:2]:
        copy.start()
    for n, (first, count) in enumerate(GROUPS):
        for f in range(first, first + count):
            pltpu.make_async_copy(
                volts_hbm.at[:, pl.ds(f * NFFT, NFFT)], volts.at[f], volts_sem.at[n]
            ).start(priority=f % 2)

    def device(i, j, d, f=0):
        return (
            lax.rem(yh + i, 2) * 4 + lax.rem(x + j, 4),
            (lax.rem(yl + f, 2) * 8 + lax.rem(z + d, 8)) * 2 + core,
        )

    c_device = (grp, blk + 1 - 2 * core)
    near = (0, 1, 7)
    direct = [
        (i, j, d, f) for i in range(2) for j in range(4) for d in near for f in range(2)
    ]
    direct.remove((0, 0, 0, 0))
    direct.sort(key=lambda m: (-hops(m[2], 8), m[3], -2 * m[0] - hops(m[1], 4)))

    barrier = pltpu.get_barrier_semaphore()
    partners = [device(*m) for m in direct] + [device(0, 0, d) for d in (2, 3, 5, 6)]
    partners.append(c_device)
    for to in partners:
        pl.semaphore_signal(barrier, inc=1, device_id=to, device_id_type=MESH)

    inputs[2].start()
    inputs[0].wait()
    factors = tables(index_ref)
    inputs[1].wait()
    form_weights(factors, taps_ref, weights)
    for n, (first, count) in enumerate(GROUPS):
        part = volts.at[pl.ds(first, count)]
        pltpu.make_async_copy(part, part, volts_sem.at[n]).wait()
        channelize(volts, weights, acc, first, count)
    pieces_of(acc, pairs, pieces)
    pl.semaphore_wait(barrier, len(partners))

    sent = []

    def send(src, s, r, to, dst=None):
        dst = src if dst is None else dst
        pltpu.make_async_remote_copy(
            src_ref=src, dst_ref=dst, send_sem=s, recv_sem=r,
            device_id=to, device_id_type=MESH,
        ).start()
        sent.append((src, s))

    def wait(ref, sem):
        pltpu.make_async_copy(ref, ref, sem).wait()

    def held(y, first, count=1):
        return buf.at[y, core, pl.ds(first, count)]

    for m in direct:
        to = device(*m)
        pltpu.make_async_remote_copy(
            src_ref=pieces.at[to[0]], dst_ref=buf.at[yl, core, PLACE[m[2]], grp],
            send_sem=s_send, recv_sem=(t_recv if m[3] else s_recv).at[m[2]],
            device_id=to, device_id_type=MESH,
        ).start()
    buf[yl, core, 0, grp] = pieces[grp]
    inputs[2].wait()
    form_onehot(order_ref, onehot)

    y_device = device(0, 0, 0, 1)
    other = 1 - yl

    def to_y(n, first, count):
        send(held(yl, first, count), y_send.at[n], y_recv.at[n], y_device)

    def to_core(n, y, first, count):
        send(held(y, first, count), c_send.at[n], c_recv.at[n], c_device)

    def from_core(n, y, first, count):
        wait(buf.at[y, 1 - core, pl.ds(first, count)], c_recv.at[n])

    def permute(d):
        permute_level(buf, PLACE[d], onehot, permuted, lax.rem(z - d + 8, 8), d == 0)

    def half(y, place, h):
        return buf.at[y, core, place, pl.ds(4 * h, 4)]

    def relay(h, y, o, steps):
        for n in steps:
            n_sem, to = 3 * h + n - 1, device(0, 0, n if h == 0 else 8 - n)
            if n == 3:
                src, dst = half(y, 1 + h, h), half(y, 7, h)
            else:
                src, dst = held(y, 1 + h), held(y, 1 + h + 2 * n)
            send(src, r_send.at[o, n_sem], r_recv.at[o, n_sem], to, dst)

    def relayed(y, o, n):
        for h in range(2):
            dst = half(y, 7, h) if n == 3 else held(y, 1 + h + 2 * n)
            wait(dst, r_recv.at[o, 3 * h + n - 1])

    for h, d in enumerate((1, 7)):
        wait(held(yl, 1 + h), s_recv.at[d])
        relay(h, yl, 0, (1, 3, 2))
    for h, d in enumerate((1, 7)):
        wait(held(other, 1 + h), t_recv.at[d])
        relay(h, other, 1, (3, 2))
    wait(buf.at[yl, core, 0, pl.ds(0, 7)], s_recv.at[0])
    to_core(0, yl, 0, 3)
    wait(held(other, 0), t_recv.at[0])
    to_core(1, other, 0, 3)
    relayed(yl, 0, 1)
    to_y(0, 3, 2)
    to_core(2, yl, 3, 2)
    from_core(0, yl, 0, 3)
    from_core(1, other, 0, 3)
    for d in near:
        permute(d)
    left_rows(buf[pl.ds(yl, 1), pl.ds(core, 1), pl.ds(0, 1)].reshape(64, 128), rows, lhs)
    pltpu.make_async_copy(lhs, lhs_hbm, lhs_sem).start()
    relayed(yl, 0, 2)
    to_core(3, yl, 5, 2)
    wait(held(other, 3, 2), y_recv.at[0])
    to_core(4, other, 3, 2)
    relayed(yl, 0, 3)
    to_core(5, yl, 7, 1)
    relayed(other, 1, 2)
    to_core(6, other, 5, 2)
    relayed(other, 1, 3)
    to_core(7, other, 7, 1)
    from_core(2, yl, 3, 2)
    from_core(4, other, 3, 2)
    permute(2)
    permute(6)
    from_core(3, yl, 5, 2)
    from_core(6, other, 5, 2)
    permute(3)
    permute(5)
    from_core(5, yl, 7, 1)
    from_core(7, other, 7, 1)
    permute(4)
    weave_columns(permuted, cols, cols_hbm, cols_sem)
    for ref, s in sent:
        wait(ref, s)
    for n in range(len(direct) // 8):
        wait(buf.at[0, 0, 0], s_send)
    wait(buf.at[0, 0, 0, pl.ds(0, len(direct) % 8)], s_send)
    wait(lhs, lhs_sem)
    wait(cols, cols_sem)


def spectra_of_all(index, taps, order, volts):
    dma = pltpu.SemaphoreType.DMA
    vmem = pltpu.VMEM
    return pl.pallas_call(
        spectra_kernel,
        out_shape=[
            jax.ShapeDtypeStruct((512, 64), BF16),
            jax.ShapeDtypeStruct((64, 4096), BF16),
        ],
        in_specs=[pl.BlockSpec(memory_space=pltpu.HBM)] * 4,
        out_specs=[pl.BlockSpec(memory_space=pltpu.HBM)] * 2,
        scratch_shapes=[
            pltpu.SMEM((16,), I32),
            vmem((TAPS, NFFT), F32),
            vmem((16, 128), I32),
            vmem((FRAMES, 16, NFFT), BF16),
            vmem((FRAMES * 16, TAPS * 32), F32),
            vmem((8, 16, 128), F32),
            vmem((8, 8, 128), F32),
            vmem((2, 2, 8, 8, 8, 128), F32),
            vmem((8, 256, 2048), BF16),
            vmem((128, 2048), F32),
            vmem((256, 128), F32),
            vmem((512, 64), BF16),
            vmem((64, 4096), BF16),
            dma((3,)), dma((len(GROUPS),)), dma, dma,
            dma, dma((8,)), dma((8,)), dma((2, 6)), dma((2, 6)),
            dma((1,)), dma((1,)), dma((8,)), dma((8,)),
            *[vmem((TAPS * 32, FORM), BF16)] * (NFFT // FORM),
        ],
        compiler_params=pltpu.CompilerParams(
            collective_id=0, has_side_effects=True, vmem_limit_bytes=63 << 20
        ),
    )(index, taps, order, volts)


def correlate_kernel(lhs_hbm, cols_hbm, out_hbm, lhs, cols, out, lhs_sem, cols_sem, out_sem):
    steps = 4096 // QBLOCK
    left = pltpu.make_async_copy(lhs_hbm, lhs, lhs_sem)
    left.start()
    right = []
    for i in range(steps):
        at = pl.ds(i * QBLOCK, QBLOCK)
        right.append(pltpu.make_async_copy(cols_hbm.at[:, at], cols.at[:, at], cols_sem.at[i]))
        right[i].start()
    left.wait()
    for i in range(steps):
        at = pl.ds(i * QBLOCK, QBLOCK)
        right[i].wait()
        for c in range(2):
            x = jnp.dot(lhs[pl.ds(c * 256, 256), :], cols[:, at], preferred_element_type=F32)
            out[i, c] = x.astype(BF16).reshape(128, 2, QBLOCK)
        pltpu.make_async_copy(out.at[i], out_hbm.at[:, :, :, at], out_sem).start()
    pltpu.make_async_copy(out, out, out_sem).wait()


def correlate(lhs, cols):
    dma = pltpu.SemaphoreType.DMA
    vmem = pltpu.VMEM
    return pl.pallas_call(
        correlate_kernel,
        out_shape=jax.ShapeDtypeStruct((2, 128, 2, 4096), BF16),
        in_specs=[pl.BlockSpec(memory_space=pltpu.HBM)] * 2,
        out_specs=pl.BlockSpec(memory_space=pltpu.HBM),
        scratch_shapes=[
            vmem((512, 64), BF16),
            vmem((64, 4096), BF16),
            vmem((4096 // QBLOCK, 2, 128, 2, QBLOCK), BF16),
            dma, dma((4096 // QBLOCK,)), dma,
        ],
        compiler_params=pltpu.CompilerParams(vmem_limit_bytes=63 << 20),
    )(lhs, cols)


def per_device(voltages, filter_taps, channel_index, antenna_slot_order):
    lhs, cols = spectra_of_all(
        channel_index, filter_taps, antenna_slot_order.reshape(16, 128), voltages
    )
    return correlate(lhs, cols)


def solution(mesh):
    in_specs = (P(("blk", "grp"), None), P(), P(), P())
    out_specs = P("grp", "blk", None, None)
    return jax.shard_map(
        per_device, mesh=mesh, in_specs=in_specs, out_specs=out_specs, check_vma=False
    )
```

```python
import functools
import math

import jax
import jax.numpy as jnp
from jax import lax
from jax.experimental import pallas as pl
from jax.experimental.pallas import tpu as pltpu
from jax.sharding import PartitionSpec as P

F32, BF16, I32 = jnp.float32, jnp.bfloat16, jnp.int32
MESH = pl.DeviceIdType.MESH
NFFT, TAPS, SPEC, FRAMES = 8192, 8, 16, 23
GROUPS = ((0, 12), (12, 11))
FORM = 1024
QBLOCK = 1024
PLACE = {0: 0, 1: 1, 7: 2, 2: 3, 6: 4, 3: 5, 5: 6, 4: 7}


def iota(shape, dim):
    return lax.broadcasted_iota(I32, shape, dim)


def cos_turns(phase):
    phase = phase & (NFFT - 1)
    fold = jnp.where(phase > NFFT // 2, NFFT - phase, phase)
    x = (NFFT // 4 - fold).astype(F32) * jnp.float32(2.0 * math.pi / NFFT)
    square = x * x
    total = jnp.full(x.shape, 1.0 / math.factorial(13), F32)
    for n in (11, 9, 7, 5, 3, 1):
        total = total * square + jnp.float32((-1) ** (n // 2) / math.factorial(n))
    return total * x


def tables(index_ref):
    shape = (32, 128)
    row, lane = iota(shape, 0), iota(shape, 1)
    channel = jnp.zeros(shape, I32)
    for c in range(16):
        channel = jnp.where(row >> 1 == c, index_ref[c], channel)
    quarter = NFFT // 4
    fine = lane * channel + (row & 1) * quarter
    coarse = (lane & 63) * channel * 128 - (lane >> 6) * quarter
    return cos_turns(fine), cos_turns(fine + quarter), cos_turns(coarse)


def form_weights(factors, taps_ref, weights):
    first, second, coarse = factors
    for block in range(NFFT // 128):
        cos_b = jnp.broadcast_to(coarse[:, block : block + 1], first.shape)
        sin_b = jnp.broadcast_to(coarse[:, 64 + block : 65 + block], first.shape)
        twiddle = (first * cos_b + second * sin_b).astype(BF16).astype(F32)
        at = pl.ds(block * 128 % FORM, 128)
        for m in range(TAPS):
            weights[block * 128 // FORM][pl.ds(m * 32, 32), at] = (
                taps_ref[pl.ds(m, 1), pl.ds(block * 128, 128)] * twiddle
            ).astype(BF16)


def channelize(volts, weights, acc, first, count):
    at = pl.ds(first * 16, count * 16)
    for n, part in enumerate(weights):
        x = lax.dot_general(
            volts[pl.ds(first, count), :, pl.ds(n * FORM, FORM)].reshape(count * 16, FORM),
            part[...],
            (((1,), (1,)), ((), ())),
            preferred_element_type=F32,
        )
        if n == 0:
            acc[at, :] = x
        else:
            acc[at, :] += x


def pieces_of(acc, pairs, pieces):
    lane = iota((16, 128), 1)
    group = lane >> 2
    sums = [
        acc[pl.ds(f * 16, 16), :128] + acc[pl.ds((f + 4) * 16, 16), 128:]
        for f in range(SPEC + 3)
    ]
    spectra = []
    for t in range(SPEC):
        x = sums[t + 3]
        for j in (2, 1, 0):
            x = jnp.where(lane < 32 * (j + 1), sums[t + j], x)
        x = x + pltpu.roll(x, 64, 1)
        spectra.append(x + pltpu.roll(x, 32, 1))
    turned = []
    for s in range(8):
        x = spectra[s]
        for q in range(1, 16):
            x = jnp.where((group & 15) == q, spectra[(q + s) % 16], x)
        turned.append(pltpu.roll(x, 4 * s, 1) if s else x)
    for g in range(8):
        x = turned[0]
        for s in range(1, 8):
            x = jnp.where(((group - g) & 7) == s, turned[s], x)
        pairs[g] = x
    low = iota((8, 128), 1) < 64
    for g in range(8):
        even = pairs[g, pl.ds(0, 8, stride=2), :]
        odd = pairs[g, pl.ds(1, 8, stride=2), :]
        pieces[g] = jnp.where(low, even, odd)


def form_onehot(order_ref, onehot):
    lane = iota((128, 128), 1)

    def step(r, _):
        slots = order_ref[pl.ds(r, 1), :].astype(F32)
        wide = jnp.broadcast_to(slots, (128, 128)).T.astype(I32)
        at = pl.ds(pl.multiple_of(r // 8 * 128, 128), 128)
        for j in range(16):
            onehot[r % 8, at, pl.ds(j * 128, 128)] = jnp.where(
                wide == lane + j * 128, 1.0, 0.0
            ).astype(BF16)
        return _

    lax.fori_loop(0, 16, step, 0)


def permute_level(buf, place, onehot, permuted, z, first):
    slots = jnp.concatenate(
        [buf[y, c, place].reshape(64, 128).astype(BF16) for y in range(2) for c in range(2)],
        axis=0,
    )
    part = lax.dot_general(
        slots, onehot[z], (((0,), (0,)), ((), ())), preferred_element_type=F32
    )
    if first:
        permuted[...] = part
    else:
        permuted[...] += part


def weave_columns(permuted, cols, cols_hbm, out_sem):
    row, col = iota((256, 256), 0), iota((256, 256), 1)
    weave = jnp.where((col >> 1) + (col & 1) * 128 == row, 1.0, 0.0).astype(BF16)
    for j in range(16):
        at = pl.ds(j * 128, 128)
        both = jnp.concatenate([permuted[:64, at], permuted[64:, at]], axis=1)
        cols[:, pl.ds(j * 256, 256)] = jnp.dot(
            both.astype(BF16), weave, preferred_element_type=F32
        ).astype(BF16)
        if j % 4 == 3:
            part = pl.ds((j - 3) * 256, 1024)
            pltpu.make_async_copy(cols.at[:, part], cols_hbm.at[:, part], out_sem).start()


def left_rows(mine, rows, lhs):
    mine = mine * jnp.float32(1.0 / SPEC)
    even = (iota((64, 128), 1) & 1) == 0
    crossed = jnp.where(even, pltpu.roll(mine, 127, 1), -pltpu.roll(mine, 1, 1))
    for o, part in enumerate((mine, crossed)):
        rows[pl.ds(o, 64, stride=4), :] = part
        rows[pl.ds(2 + o, 64, stride=4), :] = pltpu.roll(part, 64, 1)
    both = rows[...]
    channel = (iota(both.shape, 1) >> 1) & 1
    for c in range(2):
        lhs[pl.ds(c * 256, 256), :] = jnp.where(channel == c, both, 0.0).astype(BF16)[:, :64]


def hops(n, size):
    return min(n % size, -n % size)


def spectra_kernel(
    index_hbm, taps_hbm, order_hbm, volts_hbm, lhs_hbm, cols_hbm,
    index_ref, taps_ref, order_ref, volts, acc, pairs, pieces, buf,
    onehot, permuted, rows, lhs, cols, in_sem, volts_sem, lhs_sem, cols_sem,
    s_send, s_recv, t_recv, r_send, r_recv, y_send, y_recv, c_send, c_recv, *weights,
):
    grp, blk = lax.axis_index("grp"), lax.axis_index("blk")
    yh, x = grp // 4, lax.rem(grp, 4)
    yl, z, core = blk // 16, lax.rem(blk // 2, 8), lax.rem(blk, 2)

    inputs = [
        pltpu.make_async_copy(a, b, in_sem.at[n])
        for n, (a, b) in enumerate(
            [(index_hbm, index_ref), (taps_hbm, taps_ref), (order_hbm, order_ref)]
        )
    ]
    for copy in inputs[:2]:
        copy.start()
    for n, (first, count) in enumerate(GROUPS):
        for f in range(first, first + count):
            pltpu.make_async_copy(
                volts_hbm.at[:, pl.ds(f * NFFT, NFFT)], volts.at[f], volts_sem.at[n]
            ).start(priority=f % 2)

    def device(i, j, d, f=0):
        return (
            lax.rem(yh + i, 2) * 4 + lax.rem(x + j, 4),
            (lax.rem(yl + f, 2) * 8 + lax.rem(z + d, 8)) * 2 + core,
        )

    c_device = (grp, blk + 1 - 2 * core)
    near = (0, 1, 7)
    direct = [
        (i, j, d, f) for i in range(2) for j in range(4) for d in near for f in range(2)
    ]
    direct.remove((0, 0, 0, 0))
    direct.sort(key=lambda m: (-hops(m[2], 8), hops(2 * m[0] + m[3], 4) + hops(m[1], 4)))

    barrier = pltpu.get_barrier_semaphore()
    partners = [device(*m) for m in direct] + [device(0, 0, d) for d in (2, 3, 5, 6)]
    partners.append(c_device)
    for to in partners:
        pl.semaphore_signal(barrier, inc=1, device_id=to, device_id_type=MESH)

    inputs[2].start()
    inputs[0].wait()
    factors = tables(index_ref)
    inputs[1].wait()
    form_weights(factors, taps_ref, weights)
    for n, (first, count) in enumerate(GROUPS):
        part = volts.at[pl.ds(first, count)]
        pltpu.make_async_copy(part, part, volts_sem.at[n]).wait()
        channelize(volts, weights, acc, first, count)
    pieces_of(acc, pairs, pieces)
    pl.semaphore_wait(barrier, len(partners))

    sent = []

    def send(src, s, r, to, dst=None):
        dst = src if dst is None else dst
        pltpu.make_async_remote_copy(
            src_ref=src, dst_ref=dst, send_sem=s, recv_sem=r,
            device_id=to, device_id_type=MESH,
        ).start()
        sent.append((src, s))

    def wait(ref, sem):
        pltpu.make_async_copy(ref, ref, sem).wait()

    def held(y, first, count=1):
        return buf.at[y, core, pl.ds(first, count)]

    for m in direct:
        to = device(*m)
        pltpu.make_async_remote_copy(
            src_ref=pieces.at[to[0]], dst_ref=buf.at[yl, core, PLACE[m[2]], grp],
            send_sem=s_send, recv_sem=(t_recv if m[3] else s_recv).at[m[0] if m[2] else 0, m[2]],
            device_id=to, device_id_type=MESH,
        ).start()
    buf[yl, core, 0, grp] = pieces[grp]
    inputs[2].wait()
    form_onehot(order_ref, onehot)

    y_device = device(0, 0, 0, 1)
    other = 1 - yl

    def to_y(n, first, count):
        send(held(yl, first, count), y_send.at[n], y_recv.at[n], y_device)

    def to_core(n, y, first, count):
        send(held(y, first, count), c_send.at[n], c_recv.at[n], c_device)

    def from_core(n, y, first, count):
        wait(buf.at[y, 1 - core, pl.ds(first, count)], c_recv.at[n])

    def permute(d):
        permute_level(buf, PLACE[d], onehot, permuted, lax.rem(z - d + 8, 8), d == 0)

    def some(y, place, i, n, h):
        row = 4 * lax.rem(yh + i, 2)
        return buf.at[y, core, place, pl.ds(row + 2 * h, 2) if n == 3 else pl.ds(row, 4)]

    def relay(h, y, o, i, steps):
        for n in steps:
            sem, to = 3 * h + n - 1, device(0, 0, n if h == 0 else 8 - n)
            src = some(y, 1 + h, i, n, h)
            dst = some(y, 7 if n == 3 else 1 + h + 2 * n, i, n, h)
            send(src, r_send.at[o, i, sem], r_recv.at[o, i, sem], to, dst)

    def relayed(y, o, n):
        for i in range(2):
            for h in range(2):
                dst = some(y, 7 if n == 3 else 1 + h + 2 * n, i, n, h)
                wait(dst, r_recv.at[o, i, 3 * h + n - 1])

    for o, i in ((0, 0), (1, 0), (1, 1), (0, 1)):
        y = other if o else yl
        for h, d in enumerate((1, 7)):
            wait(some(y, 1 + h, i, 0, h), (t_recv if o else s_recv).at[i, d])
            relay(h, y, o, i, (3, 2) if o else (1, 3, 2))
    wait(buf.at[yl, core, 0, pl.ds(0, 7)], s_recv.at[0, 0])
    to_core(0, yl, 0, 3)
    wait(held(other, 0), t_recv.at[0, 0])
    to_core(1, other, 0, 3)
    relayed(yl, 0, 1)
    to_y(0, 3, 2)
    to_core(2, yl, 3, 2)
    from_core(0, yl, 0, 3)
    from_core(1, other, 0, 3)
    for d in near:
        permute(d)
    left_rows(buf[pl.ds(yl, 1), pl.ds(core, 1), pl.ds(0, 1)].reshape(64, 128), rows, lhs)
    pltpu.make_async_copy(lhs, lhs_hbm, lhs_sem).start()
    relayed(yl, 0, 2)
    to_core(3, yl, 5, 2)
    wait(held(other, 3, 2), y_recv.at[0])
    to_core(4, other, 3, 2)
    relayed(yl, 0, 3)
    to_core(5, yl, 7, 1)
    relayed(other, 1, 2)
    to_core(6, other, 5, 2)
    relayed(other, 1, 3)
    to_core(7, other, 7, 1)
    from_core(2, yl, 3, 2)
    from_core(4, other, 3, 2)
    permute(2)
    permute(6)
    from_core(3, yl, 5, 2)
    from_core(6, other, 5, 2)
    permute(3)
    permute(5)
    from_core(5, yl, 7, 1)
    from_core(7, other, 7, 1)
    permute(4)
    weave_columns(permuted, cols, cols_hbm, cols_sem)
    for ref, s in sent:
        wait(ref, s)
    for n in range(len(direct) // 8):
        wait(buf.at[0, 0, 0], s_send)
    wait(buf.at[0, 0, 0, pl.ds(0, len(direct) % 8)], s_send)
    wait(lhs, lhs_sem)
    wait(cols, cols_sem)


def spectra_of_all(index, taps, order, volts):
    dma = pltpu.SemaphoreType.DMA
    vmem = pltpu.VMEM
    return pl.pallas_call(
        spectra_kernel,
        out_shape=[
            jax.ShapeDtypeStruct((512, 64), BF16),
            jax.ShapeDtypeStruct((64, 4096), BF16),
        ],
        in_specs=[pl.BlockSpec(memory_space=pltpu.HBM)] * 4,
        out_specs=[pl.BlockSpec(memory_space=pltpu.HBM)] * 2,
        scratch_shapes=[
            pltpu.SMEM((16,), I32),
            vmem((TAPS, NFFT), F32),
            vmem((16, 128), I32),
            vmem((FRAMES, 16, NFFT), BF16),
            vmem((FRAMES * 16, TAPS * 32), F32),
            vmem((8, 16, 128), F32),
            vmem((8, 8, 128), F32),
            vmem((2, 2, 8, 8, 8, 128), F32),
            vmem((8, 256, 2048), BF16),
            vmem((128, 2048), F32),
            vmem((256, 128), F32),
            vmem((512, 64), BF16),
            vmem((64, 4096), BF16),
            dma((3,)), dma((len(GROUPS),)), dma, dma,
            dma, dma((2, 8)), dma((2, 8)), dma((2, 2, 6)), dma((2, 2, 6)),
            dma((1,)), dma((1,)), dma((8,)), dma((8,)),
            *[vmem((TAPS * 32, FORM), BF16)] * (NFFT // FORM),
        ],
        compiler_params=pltpu.CompilerParams(
            collective_id=0, has_side_effects=True, vmem_limit_bytes=63 << 20
        ),
    )(index, taps, order, volts)


def correlate_kernel(lhs_hbm, cols_hbm, out_hbm, lhs, cols, out, lhs_sem, cols_sem, out_sem):
    steps = 4096 // QBLOCK
    left = pltpu.make_async_copy(lhs_hbm, lhs, lhs_sem)
    left.start()
    right = []
    for i in range(steps):
        at = pl.ds(i * QBLOCK, QBLOCK)
        right.append(pltpu.make_async_copy(cols_hbm.at[:, at], cols.at[:, at], cols_sem.at[i]))
        right[i].start()
    left.wait()
    for i in range(steps):
        at = pl.ds(i * QBLOCK, QBLOCK)
        right[i].wait()
        for c in range(2):
            x = jnp.dot(lhs[pl.ds(c * 256, 256), :], cols[:, at], preferred_element_type=F32)
            out[i, c] = x.astype(BF16).reshape(128, 2, QBLOCK)
        pltpu.make_async_copy(out.at[i], out_hbm.at[:, :, :, at], out_sem).start()
    pltpu.make_async_copy(out, out, out_sem).wait()


def correlate(lhs, cols):
    dma = pltpu.SemaphoreType.DMA
    vmem = pltpu.VMEM
    return pl.pallas_call(
        correlate_kernel,
        out_shape=jax.ShapeDtypeStruct((2, 128, 2, 4096), BF16),
        in_specs=[pl.BlockSpec(memory_space=pltpu.HBM)] * 2,
        out_specs=pl.BlockSpec(memory_space=pltpu.HBM),
        scratch_shapes=[
            vmem((512, 64), BF16),
            vmem((64, 4096), BF16),
            vmem((4096 // QBLOCK, 2, 128, 2, QBLOCK), BF16),
            dma, dma((4096 // QBLOCK,)), dma,
        ],
        compiler_params=pltpu.CompilerParams(vmem_limit_bytes=63 << 20),
    )(lhs, cols)


def per_device(voltages, filter_taps, channel_index, antenna_slot_order):
    lhs, cols = spectra_of_all(
        channel_index, filter_taps, antenna_slot_order.reshape(16, 128), voltages
    )
    return correlate(lhs, cols)


def solution(mesh):
    in_specs = (P(("blk", "grp"), None), P(), P(), P())
    out_specs = P("grp", "blk", None, None)
    return jax.shard_map(
        per_device, mesh=mesh, in_specs=in_specs, out_specs=out_specs, check_vma=False
    )
```

```python
import functools
import math

import jax
import jax.numpy as jnp
from jax import lax
from jax.experimental import pallas as pl
from jax.experimental.pallas import tpu as pltpu
from jax.sharding import PartitionSpec as P

F32, BF16, I32 = jnp.float32, jnp.bfloat16, jnp.int32
MESH = pl.DeviceIdType.MESH
NFFT, TAPS, SPEC, FRAMES = 8192, 8, 16, 23
GROUPS = ((0, 10), (10, 8), (18, 5))
FORM = 1024
QBLOCK = 2048
PLACE = {0: 0, 1: 1, 7: 2, 2: 3, 6: 4, 3: 5, 5: 6, 4: 7}


def iota(shape, dim):
    return lax.broadcasted_iota(I32, shape, dim)


def cos_turns(phase):
    phase = phase & (NFFT - 1)
    fold = jnp.where(phase > NFFT // 2, NFFT - phase, phase)
    x = (NFFT // 4 - fold).astype(F32) * jnp.float32(2.0 * math.pi / NFFT)
    square = x * x
    total = jnp.full(x.shape, 1.0 / math.factorial(13), F32)
    for n in (11, 9, 7, 5, 3, 1):
        total = total * square + jnp.float32((-1) ** (n // 2) / math.factorial(n))
    return total * x


def tables(index_ref):
    shape = (32, 128)
    row, lane = iota(shape, 0), iota(shape, 1)
    channel = jnp.zeros(shape, I32)
    for c in range(16):
        channel = jnp.where(row >> 1 == c, index_ref[c], channel)
    quarter = NFFT // 4
    fine = lane * channel + (row & 1) * quarter
    coarse = (lane & 63) * channel * 128 - (lane >> 6) * quarter
    return cos_turns(fine), cos_turns(fine + quarter), cos_turns(coarse)


def form_weights(factors, taps_ref, weights):
    first, second, coarse = factors
    for block in range(NFFT // 128):
        cos_b = jnp.broadcast_to(coarse[:, block : block + 1], first.shape)
        sin_b = jnp.broadcast_to(coarse[:, 64 + block : 65 + block], first.shape)
        twiddle = (first * cos_b + second * sin_b).astype(BF16).astype(F32)
        at = pl.ds(block * 128 % FORM, 128)
        for m in range(TAPS):
            weights[block * 128 // FORM][pl.ds(m * 32, 32), at] = (
                taps_ref[pl.ds(m, 1), pl.ds(block * 128, 128)] * twiddle
            ).astype(BF16)


def channelize(volts, weights, acc, first, count):
    at = pl.ds(first * 16, count * 16)
    for n, part in enumerate(weights):
        x = lax.dot_general(
            volts[pl.ds(first, count), :, pl.ds(n * FORM, FORM)].reshape(count * 16, FORM),
            part[...],
            (((1,), (1,)), ((), ())),
            preferred_element_type=F32,
        )
        if n == 0:
            acc[at, :] = x
        else:
            acc[at, :] += x


def pieces_of(acc, pairs, pieces):
    lane = iota((16, 128), 1)
    group = lane >> 2
    sums = [
        acc[pl.ds(f * 16, 16), :128] + acc[pl.ds((f + 4) * 16, 16), 128:]
        for f in range(SPEC + 3)
    ]
    spectra = []
    for t in range(SPEC):
        x = sums[t + 3]
        for j in (2, 1, 0):
            x = jnp.where(lane < 32 * (j + 1), sums[t + j], x)
        x = x + pltpu.roll(x, 64, 1)
        spectra.append(x + pltpu.roll(x, 32, 1))
    turned = []
    for s in range(8):
        x = spectra[s]
        for q in range(1, 16):
            x = jnp.where((group & 15) == q, spectra[(q + s) % 16], x)
        turned.append(pltpu.roll(x, 4 * s, 1) if s else x)
    for g in range(8):
        x = turned[0]
        for s in range(1, 8):
            x = jnp.where(((group - g) & 7) == s, turned[s], x)
        pairs[g] = x
    low = iota((8, 128), 1) < 64
    for g in range(8):
        even = pairs[g, pl.ds(0, 8, stride=2), :]
        odd = pairs[g, pl.ds(1, 8, stride=2), :]
        pieces[g] = jnp.where(low, even, odd)


def form_onehot(order_ref, onehot):
    lane = iota((128, 128), 1)

    def step(r, _):
        slots = order_ref[pl.ds(r, 1), :].astype(F32)
        wide = jnp.broadcast_to(slots, (128, 128)).T.astype(I32)
        at = pl.ds(pl.multiple_of(r // 8 * 128, 128), 128)
        for j in range(16):
            onehot[r % 8, at, pl.ds(j * 128, 128)] = jnp.where(
                wide == lane + j * 128, 1.0, 0.0
            ).astype(BF16)
        return _

    lax.fori_loop(0, 16, step, 0)


def permute_level(buf, place, onehot, permuted, z, first):
    slots = jnp.concatenate(
        [buf[y, c, place].reshape(64, 128).astype(BF16) for y in range(2) for c in range(2)],
        axis=0,
    )
    part = lax.dot_general(
        slots, onehot[z], (((0,), (0,)), ((), ())), preferred_element_type=F32
    )
    if first:
        permuted[...] = part
    else:
        permuted[...] += part


def weave_columns(permuted, cols, cols_hbm, out_sem):
    row, col = iota((256, 256), 0), iota((256, 256), 1)
    weave = jnp.where((col >> 1) + (col & 1) * 128 == row, 1.0, 0.0).astype(BF16)
    for j in range(16):
        at = pl.ds(j * 128, 128)
        both = jnp.concatenate([permuted[:64, at], permuted[64:, at]], axis=1)
        cols[:, pl.ds(j * 256, 256)] = jnp.dot(
            both.astype(BF16), weave, preferred_element_type=F32
        ).astype(BF16)
        if j % 4 == 3:
            part = pl.ds((j - 3) * 256, 1024)
            pltpu.make_async_copy(cols.at[:, part], cols_hbm.at[:, part], out_sem).start()


def left_rows(mine, rows, lhs):
    mine = mine * jnp.float32(1.0 / SPEC)
    even = (iota((64, 128), 1) & 1) == 0
    crossed = jnp.where(even, pltpu.roll(mine, 127, 1), -pltpu.roll(mine, 1, 1))
    for o, part in enumerate((mine, crossed)):
        rows[pl.ds(o, 64, stride=4), :] = part
        rows[pl.ds(2 + o, 64, stride=4), :] = pltpu.roll(part, 64, 1)
    both = rows[...]
    channel = (iota(both.shape, 1) >> 1) & 1
    for c in range(2):
        lhs[pl.ds(c * 256, 256), :] = jnp.where(channel == c, both, 0.0).astype(BF16)[:, :64]


def hops(n, size):
    return min(n % size, -n % size)


def spectra_kernel(
    index_hbm, taps_hbm, order_hbm, volts_hbm, lhs_hbm, cols_hbm,
    index_ref, taps_ref, order_ref, volts, acc, pairs, pieces, buf,
    onehot, permuted, rows, lhs, cols, in_sem, volts_sem, lhs_sem, cols_sem,
    s_send, s_recv, t_recv, r_send, r_recv, y_send, y_recv, c_send, c_recv, *weights,
):
    grp, blk = lax.axis_index("grp"), lax.axis_index("blk")
    yh, x = grp // 4, lax.rem(grp, 4)
    yl, z, core = blk // 16, lax.rem(blk // 2, 8), lax.rem(blk, 2)

    inputs = [
        pltpu.make_async_copy(a, b, in_sem.at[n])
        for n, (a, b) in enumerate(
            [(index_hbm, index_ref), (taps_hbm, taps_ref), (order_hbm, order_ref)]
        )
    ]
    for copy in inputs[:2]:
        copy.start()
    for n, (first, count) in enumerate(GROUPS):
        for f in range(first, first + count):
            pltpu.make_async_copy(
                volts_hbm.at[:, pl.ds(f * NFFT, NFFT)], volts.at[f], volts_sem.at[n]
            ).start(priority=f % 2)

    def device(i, j, d, f=0):
        return (
            lax.rem(yh + i, 2) * 4 + lax.rem(x + j, 4),
            (lax.rem(yl + f, 2) * 8 + lax.rem(z + d, 8)) * 2 + core,
        )

    c_device = (grp, blk + 1 - 2 * core)
    near = (0, 1, 7)
    direct = [
        (i, j, d, f) for i in range(2) for j in range(4) for d in near for f in range(2)
    ]
    direct.remove((0, 0, 0, 0))
    direct.sort(key=lambda m: (-hops(m[2], 8), m[3], -2 * m[0] - hops(m[1], 4)))

    barrier = pltpu.get_barrier_semaphore()
    partners = [device(*m) for m in direct] + [device(0, 0, d) for d in (2, 3, 5, 6)]
    partners.append(c_device)
    for to in partners:
        pl.semaphore_signal(barrier, inc=1, device_id=to, device_id_type=MESH)

    inputs[2].start()
    inputs[0].wait()
    factors = tables(index_ref)
    inputs[1].wait()
    form_weights(factors, taps_ref, weights)
    for n, (first, count) in enumerate(GROUPS):
        part = volts.at[pl.ds(first, count)]
        pltpu.make_async_copy(part, part, volts_sem.at[n]).wait()
        channelize(volts, weights, acc, first, count)
    pieces_of(acc, pairs, pieces)
    pl.semaphore_wait(barrier, len(partners))

    sent = []

    def send(src, s, r, to, dst=None):
        dst = src if dst is None else dst
        pltpu.make_async_remote_copy(
            src_ref=src, dst_ref=dst, send_sem=s, recv_sem=r,
            device_id=to, device_id_type=MESH,
        ).start()
        sent.append((src, s))

    def wait(ref, sem):
        pltpu.make_async_copy(ref, ref, sem).wait()

    def held(y, first, count=1):
        return buf.at[y, core, pl.ds(first, count)]

    for m in direct:
        to = device(*m)
        pltpu.make_async_remote_copy(
            src_ref=pieces.at[to[0]], dst_ref=buf.at[yl, core, PLACE[m[2]], grp],
            send_sem=s_send, recv_sem=(t_recv if m[3] else s_recv).at[m[2]],
            device_id=to, device_id_type=MESH,
        ).start()
    buf[yl, core, 0, grp] = pieces[grp]
    inputs[2].wait()
    form_onehot(order_ref, onehot)

    y_device = device(0, 0, 0, 1)
    other = 1 - yl

    def to_y(n, first, count):
        send(held(yl, first, count), y_send.at[n], y_recv.at[n], y_device)

    def to_core(n, y, first, count):
        send(held(y, first, count), c_send.at[n], c_recv.at[n], c_device)

    def from_core(n, y, first, count):
        wait(buf.at[y, 1 - core, pl.ds(first, count)], c_recv.at[n])

    def permute(d):
        permute_level(buf, PLACE[d], onehot, permuted, lax.rem(z - d + 8, 8), d == 0)

    def half(y, place, h):
        return buf.at[y, core, place, pl.ds(4 * h, 4)]

    def relay(h, y, o, steps):
        for n in steps:
            n_sem, to = 3 * h + n - 1, device(0, 0, n if h == 0 else 8 - n)
            if n == 3:
                src, dst = half(y, 1 + h, h), half(y, 7, h)
            else:
                src, dst = held(y, 1 + h), held(y, 1 + h + 2 * n)
            send(src, r_send.at[o, n_sem], r_recv.at[o, n_sem], to, dst)

    def relayed(y, o, n):
        for h in range(2):
            dst = half(y, 7, h) if n == 3 else held(y, 1 + h + 2 * n)
            wait(dst, r_recv.at[o, 3 * h + n - 1])

    for h, d in enumerate((1, 7)):
        wait(held(yl, 1 + h), s_recv.at[d])
        relay(h, yl, 0, (1, 2, 3))
    for h, d in enumerate((1, 7)):
        wait(held(other, 1 + h), t_recv.at[d])
        relay(h, other, 1, (2, 3))
    wait(buf.at[yl, core, 0, pl.ds(0, 7)], s_recv.at[0])
    to_core(0, yl, 0, 3)
    wait(held(other, 0), t_recv.at[0])
    to_core(1, other, 0, 3)
    relayed(yl, 0, 1)
    to_y(0, 3, 2)
    to_core(2, yl, 3, 2)
    from_core(0, yl, 0, 3)
    from_core(1, other, 0, 3)
    for d in near:
        permute(d)
    left_rows(buf[pl.ds(yl, 1), pl.ds(core, 1), pl.ds(0, 1)].reshape(64, 128), rows, lhs)
    pltpu.make_async_copy(lhs, lhs_hbm, lhs_sem).start()
    relayed(yl, 0, 2)
    to_core(3, yl, 5, 2)
    wait(held(other, 3, 2), y_recv.at[0])
    to_core(4, other, 3, 2)
    relayed(yl, 0, 3)
    to_core(5, yl, 7, 1)
    relayed(other, 1, 2)
    to_core(6, other, 5, 2)
    relayed(other, 1, 3)
    to_core(7, other, 7, 1)
    from_core(2, yl, 3, 2)
    from_core(4, other, 3, 2)
    permute(2)
    permute(6)
    from_core(3, yl, 5, 2)
    from_core(6, other, 5, 2)
    permute(3)
    permute(5)
    from_core(5, yl, 7, 1)
    from_core(7, other, 7, 1)
    permute(4)
    weave_columns(permuted, cols, cols_hbm, cols_sem)
    for ref, s in sent:
        wait(ref, s)
    for n in range(len(direct) // 8):
        wait(buf.at[0, 0, 0], s_send)
    wait(buf.at[0, 0, 0, pl.ds(0, len(direct) % 8)], s_send)
    wait(lhs, lhs_sem)
    wait(cols, cols_sem)


def spectra_of_all(index, taps, order, volts):
    dma = pltpu.SemaphoreType.DMA
    vmem = pltpu.VMEM
    return pl.pallas_call(
        spectra_kernel,
        out_shape=[
            jax.ShapeDtypeStruct((512, 64), BF16),
            jax.ShapeDtypeStruct((64, 4096), BF16),
        ],
        in_specs=[pl.BlockSpec(memory_space=pltpu.HBM)] * 4,
        out_specs=[pl.BlockSpec(memory_space=pltpu.HBM)] * 2,
        scratch_shapes=[
            pltpu.SMEM((16,), I32),
            vmem((TAPS, NFFT), F32),
            vmem((16, 128), I32),
            vmem((FRAMES, 16, NFFT), BF16),
            vmem((FRAMES * 16, TAPS * 32), F32),
            vmem((8, 16, 128), F32),
            vmem((8, 8, 128), F32),
            vmem((2, 2, 8, 8, 8, 128), F32),
            vmem((8, 256, 2048), BF16),
            vmem((128, 2048), F32),
            vmem((256, 128), F32),
            vmem((512, 64), BF16),
            vmem((64, 4096), BF16),
            dma((3,)), dma((len(GROUPS),)), dma, dma,
            dma, dma((8,)), dma((8,)), dma((2, 6)), dma((2, 6)),
            dma((1,)), dma((1,)), dma((8,)), dma((8,)),
            *[vmem((TAPS * 32, FORM), BF16)] * (NFFT // FORM),
        ],
        compiler_params=pltpu.CompilerParams(
            collective_id=0, has_side_effects=True, vmem_limit_bytes=63 << 20
        ),
    )(index, taps, order, volts)


def correlate_kernel(lhs_hbm, cols_hbm, out_hbm, lhs, cols, out, lhs_sem, cols_sem, out_sem):
    steps = 4096 // QBLOCK
    left = pltpu.make_async_copy(lhs_hbm, lhs, lhs_sem)
    left.start()
    right = []
    for i in range(steps):
        at = pl.ds(i * QBLOCK, QBLOCK)
        right.append(pltpu.make_async_copy(cols_hbm.at[:, at], cols.at[:, at], cols_sem.at[i]))
        right[i].start()
    left.wait()
    for i in range(steps):
        at = pl.ds(i * QBLOCK, QBLOCK)
        right[i].wait()
        for c in range(2):
            x = jnp.dot(lhs[pl.ds(c * 256, 256), :], cols[:, at], preferred_element_type=F32)
            out[i, c] = x.astype(BF16).reshape(128, 2, QBLOCK)
            pltpu.make_async_copy(
                out.at[i, c], out_hbm.at[c, :, :, at], out_sem.at[i, c]
            ).start(priority=c)
    for i in range(steps):
        for c in range(2):
            pltpu.make_async_copy(out.at[i, c], out.at[i, c], out_sem.at[i, c]).wait()


def correlate(lhs, cols):
    dma = pltpu.SemaphoreType.DMA
    vmem = pltpu.VMEM
    return pl.pallas_call(
        correlate_kernel,
        out_shape=jax.ShapeDtypeStruct((2, 128, 2, 4096), BF16),
        in_specs=[pl.BlockSpec(memory_space=pltpu.HBM)] * 2,
        out_specs=pl.BlockSpec(memory_space=pltpu.HBM),
        scratch_shapes=[
            vmem((512, 64), BF16),
            vmem((64, 4096), BF16),
            vmem((4096 // QBLOCK, 2, 128, 2, QBLOCK), BF16),
            dma, dma((4096 // QBLOCK,)), dma((4096 // QBLOCK, 2)),
        ],
        compiler_params=pltpu.CompilerParams(vmem_limit_bytes=63 << 20),
    )(lhs, cols)


def per_device(voltages, filter_taps, channel_index, antenna_slot_order):
    lhs, cols = spectra_of_all(
        channel_index, filter_taps, antenna_slot_order.reshape(16, 128), voltages
    )
    return correlate(lhs, cols)


def solution(mesh):
    in_specs = (P(("blk", "grp"), None), P(), P(), P())
    out_specs = P("grp", "blk", None, None)
    return jax.shard_map(
        per_device, mesh=mesh, in_specs=in_specs, out_specs=out_specs, check_vma=False
    )
```

```python
import functools
import math

import jax
import jax.numpy as jnp
from jax import lax
from jax.experimental import pallas as pl
from jax.experimental.pallas import tpu as pltpu
from jax.sharding import PartitionSpec as P

F32, BF16, I32 = jnp.float32, jnp.bfloat16, jnp.int32
MESH = pl.DeviceIdType.MESH
NFFT, TAPS, SPEC, FRAMES = 8192, 8, 16, 23
GROUPS = ((0, 23),)
FORM = 1024
QBLOCK = 2048
PLACE = {0: 0, 1: 1, 7: 2, 2: 3, 6: 4, 3: 5, 5: 6, 4: 7}


def iota(shape, dim):
    return lax.broadcasted_iota(I32, shape, dim)


def cos_turns(phase):
    phase = phase & (NFFT - 1)
    fold = jnp.where(phase > NFFT // 2, NFFT - phase, phase)
    x = (NFFT // 4 - fold).astype(F32) * jnp.float32(2.0 * math.pi / NFFT)
    square = x * x
    total = jnp.full(x.shape, 1.0 / math.factorial(13), F32)
    for n in (11, 9, 7, 5, 3, 1):
        total = total * square + jnp.float32((-1) ** (n // 2) / math.factorial(n))
    return total * x


def tables(index_ref):
    shape = (32, 128)
    row, lane = iota(shape, 0), iota(shape, 1)
    channel = jnp.zeros(shape, I32)
    for c in range(16):
        channel = jnp.where(row >> 1 == c, index_ref[c], channel)
    quarter = NFFT // 4
    fine = lane * channel + (row & 1) * quarter
    coarse = (lane & 63) * channel * 128 - (lane >> 6) * quarter
    return cos_turns(fine), cos_turns(fine + quarter), cos_turns(coarse)


def form_weights(factors, taps_ref, weights):
    first, second, coarse = factors
    for block in range(NFFT // 128):
        cos_b = jnp.broadcast_to(coarse[:, block : block + 1], first.shape)
        sin_b = jnp.broadcast_to(coarse[:, 64 + block : 65 + block], first.shape)
        twiddle = (first * cos_b + second * sin_b).astype(BF16).astype(F32)
        at = pl.ds(block * 128 % FORM, 128)
        for m in range(TAPS):
            weights[block * 128 // FORM][pl.ds(m * 32, 32), at] = (
                taps_ref[pl.ds(m, 1), pl.ds(block * 128, 128)] * twiddle
            ).astype(BF16)


def channelize(volts, weights, acc, first, count):
    at = pl.ds(first * 16, count * 16)
    for n, part in enumerate(weights):
        x = lax.dot_general(
            volts[pl.ds(first, count), :, pl.ds(n * FORM, FORM)].reshape(count * 16, FORM),
            part[...],
            (((1,), (1,)), ((), ())),
            preferred_element_type=F32,
        )
        if n == 0:
            acc[at, :] = x
        else:
            acc[at, :] += x


def pieces_of(acc, pairs, pieces):
    lane = iota((16, 128), 1)
    group = lane >> 2
    sums = [
        acc[pl.ds(f * 16, 16), :128] + acc[pl.ds((f + 4) * 16, 16), 128:]
        for f in range(SPEC + 3)
    ]
    spectra = []
    for t in range(SPEC):
        x = sums[t + 3]
        for j in (2, 1, 0):
            x = jnp.where(lane < 32 * (j + 1), sums[t + j], x)
        x = x + pltpu.roll(x, 64, 1)
        spectra.append(x + pltpu.roll(x, 32, 1))
    turned = []
    for s in range(8):
        x = spectra[s]
        for q in range(1, 16):
            x = jnp.where((group & 15) == q, spectra[(q + s) % 16], x)
        turned.append(pltpu.roll(x, 4 * s, 1) if s else x)
    for g in range(8):
        x = turned[0]
        for s in range(1, 8):
            x = jnp.where(((group - g) & 7) == s, turned[s], x)
        pairs[g] = x
    low = iota((8, 128), 1) < 64
    for g in range(8):
        even = pairs[g, pl.ds(0, 8, stride=2), :]
        odd = pairs[g, pl.ds(1, 8, stride=2), :]
        pieces[g] = jnp.where(low, even, odd)


def form_onehot(order_ref, onehot):
    lane = iota((128, 128), 1)

    def step(r, _):
        slots = order_ref[pl.ds(r, 1), :].astype(F32)
        wide = jnp.broadcast_to(slots, (128, 128)).T.astype(I32)
        at = pl.ds(pl.multiple_of(r // 8 * 128, 128), 128)
        for j in range(16):
            onehot[r % 8, at, pl.ds(j * 128, 128)] = jnp.where(
                wide == lane + j * 128, 1.0, 0.0
            ).astype(BF16)
        return _

    lax.fori_loop(0, 16, step, 0)


def permute_level(buf, place, onehot, permuted, z, first):
    slots = jnp.concatenate(
        [buf[y, c, place].reshape(64, 128).astype(BF16) for y in range(2) for c in range(2)],
        axis=0,
    )
    part = lax.dot_general(
        slots, onehot[z], (((0,), (0,)), ((), ())), preferred_element_type=F32
    )
    if first:
        permuted[...] = part
    else:
        permuted[...] += part


def weave_columns(permuted, cols, cols_hbm, out_sem):
    row, col = iota((256, 256), 0), iota((256, 256), 1)
    weave = jnp.where((col >> 1) + (col & 1) * 128 == row, 1.0, 0.0).astype(BF16)
    for j in range(16):
        at = pl.ds(j * 128, 128)
        both = jnp.concatenate([permuted[:64, at], permuted[64:, at]], axis=1)
        cols[:, pl.ds(j * 256, 256)] = jnp.dot(
            both.astype(BF16), weave, preferred_element_type=F32
        ).astype(BF16)
        if j % 4 == 3:
            part = pl.ds((j - 3) * 256, 1024)
            pltpu.make_async_copy(cols.at[:, part], cols_hbm.at[:, part], out_sem).start()


def left_rows(mine, rows, lhs):
    mine = mine * jnp.float32(1.0 / SPEC)
    even = (iota((64, 128), 1) & 1) == 0
    crossed = jnp.where(even, pltpu.roll(mine, 127, 1), -pltpu.roll(mine, 1, 1))
    for o, part in enumerate((mine, crossed)):
        rows[pl.ds(o, 64, stride=4), :] = part
        rows[pl.ds(2 + o, 64, stride=4), :] = pltpu.roll(part, 64, 1)
    both = rows[...]
    channel = (iota(both.shape, 1) >> 1) & 1
    for c in range(2):
        lhs[pl.ds(c * 256, 256), :] = jnp.where(channel == c, both, 0.0).astype(BF16)[:, :64]


def hops(n, size):
    return min(n % size, -n % size)


def spectra_kernel(
    index_hbm, taps_hbm, order_hbm, volts_hbm, lhs_hbm, cols_hbm,
    index_ref, taps_ref, order_ref, volts, acc, pairs, pieces, buf,
    onehot, permuted, rows, lhs, cols, in_sem, volts_sem, lhs_sem, cols_sem,
    s_send, s_recv, t_recv, r_send, r_recv, y_send, y_recv, c_send, c_recv, *weights,
):
    grp, blk = lax.axis_index("grp"), lax.axis_index("blk")
    yh, x = grp // 4, lax.rem(grp, 4)
    yl, z, core = blk // 16, lax.rem(blk // 2, 8), lax.rem(blk, 2)

    inputs = [
        pltpu.make_async_copy(a, b, in_sem.at[n])
        for n, (a, b) in enumerate(
            [(index_hbm, index_ref), (taps_hbm, taps_ref), (order_hbm, order_ref)]
        )
    ]
    for copy in inputs[:2]:
        copy.start()
    for n, (first, count) in enumerate(GROUPS):
        for f in range(first, first + count):
            pltpu.make_async_copy(
                volts_hbm.at[:, pl.ds(f * NFFT, NFFT)], volts.at[f], volts_sem.at[n]
            ).start(priority=f % 2)

    def device(i, j, d, f=0):
        return (
            lax.rem(yh + i, 2) * 4 + lax.rem(x + j, 4),
            (lax.rem(yl + f, 2) * 8 + lax.rem(z + d, 8)) * 2 + core,
        )

    c_device = (grp, blk + 1 - 2 * core)
    near = (0, 1, 7)
    direct = [
        (i, j, d, f) for i in range(2) for j in range(4) for d in near for f in range(2)
    ]
    direct.remove((0, 0, 0, 0))
    direct.sort(key=lambda m: (-hops(m[2], 8), m[3], -2 * m[0] - hops(m[1], 4)))

    barrier = pltpu.get_barrier_semaphore()
    partners = [device(*m) for m in direct] + [device(0, 0, d) for d in (2, 3, 5, 6)]
    partners.append(c_device)
    for to in partners:
        pl.semaphore_signal(barrier, inc=1, device_id=to, device_id_type=MESH)

    inputs[2].start()
    inputs[0].wait()
    factors = tables(index_ref)
    inputs[1].wait()
    form_weights(factors, taps_ref, weights)
    for n, (first, count) in enumerate(GROUPS):
        part = volts.at[pl.ds(first, count)]
        pltpu.make_async_copy(part, part, volts_sem.at[n]).wait()
        channelize(volts, weights, acc, first, count)
    pieces_of(acc, pairs, pieces)
    pl.semaphore_wait(barrier, len(partners))

    sent = []

    def send(src, s, r, to, dst=None):
        dst = src if dst is None else dst
        pltpu.make_async_remote_copy(
            src_ref=src, dst_ref=dst, send_sem=s, recv_sem=r,
            device_id=to, device_id_type=MESH,
        ).start()
        sent.append((src, s))

    def wait(ref, sem):
        pltpu.make_async_copy(ref, ref, sem).wait()

    def held(y, first, count=1):
        return buf.at[y, core, pl.ds(first, count)]

    for m in direct:
        to = device(*m)
        pltpu.make_async_remote_copy(
            src_ref=pieces.at[to[0]], dst_ref=buf.at[yl, core, PLACE[m[2]], grp],
            send_sem=s_send, recv_sem=(t_recv if m[3] else s_recv).at[m[2]],
            device_id=to, device_id_type=MESH,
        ).start()
    buf[yl, core, 0, grp] = pieces[grp]
    inputs[2].wait()
    form_onehot(order_ref, onehot)

    y_device = device(0, 0, 0, 1)
    other = 1 - yl

    def to_y(n, first, count):
        send(held(yl, first, count), y_send.at[n], y_recv.at[n], y_device)

    def to_core(n, y, first, count):
        send(held(y, first, count), c_send.at[n], c_recv.at[n], c_device)

    def from_core(n, y, first, count):
        wait(buf.at[y, 1 - core, pl.ds(first, count)], c_recv.at[n])

    def permute(d):
        permute_level(buf, PLACE[d], onehot, permuted, lax.rem(z - d + 8, 8), d == 0)

    def half(y, place, h):
        return buf.at[y, core, place, pl.ds(4 * h, 4)]

    def relay(h, y, o, steps):
        for n in steps:
            n_sem, to = 3 * h + n - 1, device(0, 0, n if h == 0 else 8 - n)
            if n == 3:
                src, dst = half(y, 1 + h, h), half(y, 7, h)
            else:
                src, dst = held(y, 1 + h), held(y, 1 + h + 2 * n)
            send(src, r_send.at[o, n_sem], r_recv.at[o, n_sem], to, dst)

    def relayed(y, o, n):
        for h in range(2):
            dst = half(y, 7, h) if n == 3 else held(y, 1 + h + 2 * n)
            wait(dst, r_recv.at[o, 3 * h + n - 1])

    for h, d in enumerate((1, 7)):
        wait(held(yl, 1 + h), s_recv.at[d])
        relay(h, yl, 0, (1, 2, 3))
    for h, d in enumerate((1, 7)):
        wait(held(other, 1 + h), t_recv.at[d])
        relay(h, other, 1, (2, 3))
    wait(buf.at[yl, core, 0, pl.ds(0, 7)], s_recv.at[0])
    to_core(0, yl, 0, 3)
    wait(held(other, 0), t_recv.at[0])
    to_core(1, other, 0, 3)
    relayed(yl, 0, 1)
    to_y(0, 3, 2)
    to_core(2, yl, 3, 2)
    from_core(0, yl, 0, 3)
    from_core(1, other, 0, 3)
    for d in near:
        permute(d)
    left_rows(buf[pl.ds(yl, 1), pl.ds(core, 1), pl.ds(0, 1)].reshape(64, 128), rows, lhs)
    pltpu.make_async_copy(lhs, lhs_hbm, lhs_sem).start()
    relayed(yl, 0, 2)
    to_core(3, yl, 5, 2)
    wait(held(other, 3, 2), y_recv.at[0])
    to_core(4, other, 3, 2)
    relayed(yl, 0, 3)
    to_core(5, yl, 7, 1)
    relayed(other, 1, 2)
    to_core(6, other, 5, 2)
    relayed(other, 1, 3)
    to_core(7, other, 7, 1)
    from_core(2, yl, 3, 2)
    from_core(4, other, 3, 2)
    permute(2)
    permute(6)
    from_core(3, yl, 5, 2)
    from_core(6, other, 5, 2)
    permute(3)
    permute(5)
    from_core(5, yl, 7, 1)
    from_core(7, other, 7, 1)
    permute(4)
    weave_columns(permuted, cols, cols_hbm, cols_sem)
    for ref, s in sent:
        wait(ref, s)
    for n in range(len(direct) // 8):
        wait(buf.at[0, 0, 0], s_send)
    wait(buf.at[0, 0, 0, pl.ds(0, len(direct) % 8)], s_send)
    wait(lhs, lhs_sem)
    wait(cols, cols_sem)


def spectra_of_all(index, taps, order, volts):
    dma = pltpu.SemaphoreType.DMA
    vmem = pltpu.VMEM
    return pl.pallas_call(
        spectra_kernel,
        out_shape=[
            jax.ShapeDtypeStruct((512, 64), BF16),
            jax.ShapeDtypeStruct((64, 4096), BF16),
        ],
        in_specs=[pl.BlockSpec(memory_space=pltpu.HBM)] * 4,
        out_specs=[pl.BlockSpec(memory_space=pltpu.HBM)] * 2,
        scratch_shapes=[
            pltpu.SMEM((16,), I32),
            vmem((TAPS, NFFT), F32),
            vmem((16, 128), I32),
            vmem((FRAMES, 16, NFFT), BF16),
            vmem((FRAMES * 16, TAPS * 32), F32),
            vmem((8, 16, 128), F32),
            vmem((8, 8, 128), F32),
            vmem((2, 2, 8, 8, 8, 128), F32),
            vmem((8, 256, 2048), BF16),
            vmem((128, 2048), F32),
            vmem((256, 128), F32),
            vmem((512, 64), BF16),
            vmem((64, 4096), BF16),
            dma((3,)), dma((len(GROUPS),)), dma, dma,
            dma, dma((8,)), dma((8,)), dma((2, 6)), dma((2, 6)),
            dma((1,)), dma((1,)), dma((8,)), dma((8,)),
            *[vmem((TAPS * 32, FORM), BF16)] * (NFFT // FORM),
        ],
        compiler_params=pltpu.CompilerParams(
            collective_id=0, has_side_effects=True, vmem_limit_bytes=63 << 20
        ),
    )(index, taps, order, volts)


def correlate_kernel(lhs_hbm, cols_hbm, out_hbm, lhs, cols, out, lhs_sem, cols_sem, out_sem):
    steps = 4096 // QBLOCK
    left = pltpu.make_async_copy(lhs_hbm, lhs, lhs_sem)
    left.start()
    right = []
    for i in range(steps):
        at = pl.ds(i * QBLOCK, QBLOCK)
        right.append(pltpu.make_async_copy(cols_hbm.at[:, at], cols.at[:, at], cols_sem.at[i]))
        right[i].start()
    left.wait()
    for i in range(steps):
        at = pl.ds(i * QBLOCK, QBLOCK)
        right[i].wait()
        for c in range(2):
            x = jnp.dot(lhs[pl.ds(c * 256, 256), :], cols[:, at], preferred_element_type=F32)
            out[i, c] = x.astype(BF16).reshape(128, 2, QBLOCK)
            pltpu.make_async_copy(
                out.at[i, c], out_hbm.at[c, :, :, at], out_sem.at[i, c]
            ).start(priority=c)
    for i in range(steps):
        for c in range(2):
            pltpu.make_async_copy(out.at[i, c], out.at[i, c], out_sem.at[i, c]).wait()


def correlate(lhs, cols):
    dma = pltpu.SemaphoreType.DMA
    vmem = pltpu.VMEM
    return pl.pallas_call(
        correlate_kernel,
        out_shape=jax.ShapeDtypeStruct((2, 128, 2, 4096), BF16),
        in_specs=[pl.BlockSpec(memory_space=pltpu.HBM)] * 2,
        out_specs=pl.BlockSpec(memory_space=pltpu.HBM),
        scratch_shapes=[
            vmem((512, 64), BF16),
            vmem((64, 4096), BF16),
            vmem((4096 // QBLOCK, 2, 128, 2, QBLOCK), BF16),
            dma, dma((4096 // QBLOCK,)), dma((4096 // QBLOCK, 2)),
        ],
        compiler_params=pltpu.CompilerParams(vmem_limit_bytes=63 << 20),
    )(lhs, cols)


def per_device(voltages, filter_taps, channel_index, antenna_slot_order):
    lhs, cols = spectra_of_all(
        channel_index, filter_taps, antenna_slot_order.reshape(16, 128), voltages
    )
    return correlate(lhs, cols)


def solution(mesh):
    in_specs = (P(("blk", "grp"), None), P(), P(), P())
    out_specs = P("grp", "blk", None, None)
    return jax.shard_map(
        per_device, mesh=mesh, in_specs=in_specs, out_specs=out_specs, check_vma=False
    )
```

```python
import functools
import math

import jax
import jax.numpy as jnp
from jax import lax
from jax.experimental import pallas as pl
from jax.experimental.pallas import tpu as pltpu
from jax.sharding import PartitionSpec as P

F32, BF16, I32 = jnp.float32, jnp.bfloat16, jnp.int32
MESH = pl.DeviceIdType.MESH
NFFT, TAPS, SPEC, FRAMES = 8192, 8, 16, 23
GROUPS = ((0, 23),)
FORM = 2048
QBLOCK = 2048
PLACE = {0: 0, 1: 1, 7: 2, 2: 3, 6: 4, 3: 5, 5: 6, 4: 7}


def iota(shape, dim):
    return lax.broadcasted_iota(I32, shape, dim)


def cos_turns(phase):
    phase = phase & (NFFT - 1)
    fold = jnp.where(phase > NFFT // 2, NFFT - phase, phase)
    x = (NFFT // 4 - fold).astype(F32) * jnp.float32(2.0 * math.pi / NFFT)
    square = x * x
    total = jnp.full(x.shape, 1.0 / math.factorial(13), F32)
    for n in (11, 9, 7, 5, 3, 1):
        total = total * square + jnp.float32((-1) ** (n // 2) / math.factorial(n))
    return total * x


def tables(index_ref):
    shape = (32, 128)
    row, lane = iota(shape, 0), iota(shape, 1)
    channel = jnp.zeros(shape, I32)
    for c in range(16):
        channel = jnp.where(row >> 1 == c, index_ref[c], channel)
    quarter = NFFT // 4
    fine = lane * channel + (row & 1) * quarter
    coarse = (lane & 63) * channel * 128 - (lane >> 6) * quarter
    return cos_turns(fine), cos_turns(fine + quarter), cos_turns(coarse)


def form_weights(factors, taps_ref, weights):
    first, second, coarse = factors
    for block in range(NFFT // 128):
        cos_b = jnp.broadcast_to(coarse[:, block : block + 1], first.shape)
        sin_b = jnp.broadcast_to(coarse[:, 64 + block : 65 + block], first.shape)
        twiddle = (first * cos_b + second * sin_b).astype(BF16).astype(F32)
        at = pl.ds(block * 128 % FORM, 128)
        for m in range(TAPS):
            weights[block * 128 // FORM][pl.ds(m * 32, 32), at] = (
                taps_ref[pl.ds(m, 1), pl.ds(block * 128, 128)] * twiddle
            ).astype(BF16)


def channelize(volts, weights, acc, first, count):
    at = pl.ds(first * 16, count * 16)
    for n, part in enumerate(weights):
        x = lax.dot_general(
            volts[pl.ds(first, count), :, pl.ds(n * FORM, FORM)].reshape(count * 16, FORM),
            part[...],
            (((1,), (1,)), ((), ())),
            preferred_element_type=F32,
        )
        if n == 0:
            acc[at, :] = x
        else:
            acc[at, :] += x


def pieces_of(acc, pairs, pieces):
    lane = iota((16, 128), 1)
    group = lane >> 2
    sums = [
        acc[pl.ds(f * 16, 16), :128] + acc[pl.ds((f + 4) * 16, 16), 128:]
        for f in range(SPEC + 3)
    ]
    spectra = []
    for t in range(SPEC):
        x = sums[t + 3]
        for j in (2, 1, 0):
            x = jnp.where(lane < 32 * (j + 1), sums[t + j], x)
        x = x + pltpu.roll(x, 64, 1)
        spectra.append(x + pltpu.roll(x, 32, 1))
    turned = []
    for s in range(8):
        x = spectra[s]
        for q in range(1, 16):
            x = jnp.where((group & 15) == q, spectra[(q + s) % 16], x)
        turned.append(pltpu.roll(x, 4 * s, 1) if s else x)
    for g in range(8):
        x = turned[0]
        for s in range(1, 8):
            x = jnp.where(((group - g) & 7) == s, turned[s], x)
        pairs[g] = x
    low = iota((8, 128), 1) < 64
    for g in range(8):
        even = pairs[g, pl.ds(0, 8, stride=2), :]
        odd = pairs[g, pl.ds(1, 8, stride=2), :]
        pieces[g] = jnp.where(low, even, odd)


def form_onehot(order_ref, onehot):
    lane = iota((128, 128), 1)

    def step(r, _):
        slots = order_ref[pl.ds(r, 1), :].astype(F32)
        wide = jnp.broadcast_to(slots, (128, 128)).T.astype(I32)
        at = pl.ds(pl.multiple_of(r // 8 * 128, 128), 128)
        for j in range(16):
            onehot[r % 8, at, pl.ds(j * 128, 128)] = jnp.where(
                wide == lane + j * 128, 1.0, 0.0
            ).astype(BF16)
        return _

    lax.fori_loop(0, 16, step, 0)


def permute_level(buf, place, onehot, permuted, z, first):
    slots = jnp.concatenate(
        [buf[y, c, place].reshape(64, 128).astype(BF16) for y in range(2) for c in range(2)],
        axis=0,
    )
    part = lax.dot_general(
        slots, onehot[z], (((0,), (0,)), ((), ())), preferred_element_type=F32
    )
    if first:
        permuted[...] = part
    else:
        permuted[...] += part


def weave_columns(permuted, cols, cols_hbm, out_sem):
    row, col = iota((256, 256), 0), iota((256, 256), 1)
    weave = jnp.where((col >> 1) + (col & 1) * 128 == row, 1.0, 0.0).astype(BF16)
    for j in range(16):
        at = pl.ds(j * 128, 128)
        both = jnp.concatenate([permuted[:64, at], permuted[64:, at]], axis=1)
        cols[:, pl.ds(j * 256, 256)] = jnp.dot(
            both.astype(BF16), weave, preferred_element_type=F32
        ).astype(BF16)
        if j % 4 == 3:
            part = pl.ds((j - 3) * 256, 1024)
            pltpu.make_async_copy(cols.at[:, part], cols_hbm.at[:, part], out_sem).start()


def left_rows(mine, rows, lhs):
    mine = mine * jnp.float32(1.0 / SPEC)
    even = (iota((64, 128), 1) & 1) == 0
    crossed = jnp.where(even, pltpu.roll(mine, 127, 1), -pltpu.roll(mine, 1, 1))
    for o, part in enumerate((mine, crossed)):
        rows[pl.ds(o, 64, stride=4), :] = part
        rows[pl.ds(2 + o, 64, stride=4), :] = pltpu.roll(part, 64, 1)
    both = rows[...]
    channel = (iota(both.shape, 1) >> 1) & 1
    for c in range(2):
        lhs[pl.ds(c * 256, 256), :] = jnp.where(channel == c, both, 0.0).astype(BF16)[:, :64]


def hops(n, size):
    return min(n % size, -n % size)


def spectra_kernel(
    index_hbm, taps_hbm, order_hbm, volts_hbm, lhs_hbm, cols_hbm,
    index_ref, taps_ref, order_ref, volts, acc, pairs, pieces, buf,
    onehot, permuted, rows, lhs, cols, in_sem, volts_sem, lhs_sem, cols_sem,
    s_send, s_recv, t_recv, r_send, r_recv, y_send, y_recv, c_send, c_recv, *weights,
):
    grp, blk = lax.axis_index("grp"), lax.axis_index("blk")
    yh, x = grp // 4, lax.rem(grp, 4)
    yl, z, core = blk // 16, lax.rem(blk // 2, 8), lax.rem(blk, 2)

    inputs = [
        pltpu.make_async_copy(a, b, in_sem.at[n])
        for n, (a, b) in enumerate(
            [(index_hbm, index_ref), (taps_hbm, taps_ref), (order_hbm, order_ref)]
        )
    ]
    for copy in inputs[:2]:
        copy.start()
    for n, (first, count) in enumerate(GROUPS):
        for f in range(first, first + count):
            pltpu.make_async_copy(
                volts_hbm.at[:, pl.ds(f * NFFT, NFFT)], volts.at[f], volts_sem.at[n]
            ).start(priority=f % 2)

    def device(i, j, d, f=0):
        return (
            lax.rem(yh + i, 2) * 4 + lax.rem(x + j, 4),
            (lax.rem(yl + f, 2) * 8 + lax.rem(z + d, 8)) * 2 + core,
        )

    c_device = (grp, blk + 1 - 2 * core)
    near = (0, 1, 7)
    direct = [
        (i, j, d, f) for i in range(2) for j in range(4) for d in near for f in range(2)
    ]
    direct.remove((0, 0, 0, 0))
    direct.sort(key=lambda m: (-hops(m[2], 8), m[3], -2 * m[0] - hops(m[1], 4)))

    barrier = pltpu.get_barrier_semaphore()
    partners = [device(*m) for m in direct] + [device(0, 0, d) for d in (2, 3, 5, 6)]
    partners.append(c_device)
    for to in partners:
        pl.semaphore_signal(barrier, inc=1, device_id=to, device_id_type=MESH)

    inputs[2].start()
    inputs[0].wait()
    factors = tables(index_ref)
    inputs[1].wait()
    form_weights(factors, taps_ref, weights)
    for n, (first, count) in enumerate(GROUPS):
        part = volts.at[pl.ds(first, count)]
        pltpu.make_async_copy(part, part, volts_sem.at[n]).wait()
        channelize(volts, weights, acc, first, count)
    pieces_of(acc, pairs, pieces)
    pl.semaphore_wait(barrier, len(partners))

    sent = []

    def send(src, s, r, to, dst=None):
        dst = src if dst is None else dst
        pltpu.make_async_remote_copy(
            src_ref=src, dst_ref=dst, send_sem=s, recv_sem=r,
            device_id=to, device_id_type=MESH,
        ).start()
        sent.append((src, s))

    def wait(ref, sem):
        pltpu.make_async_copy(ref, ref, sem).wait()

    def held(y, first, count=1):
        return buf.at[y, core, pl.ds(first, count)]

    for m in direct:
        to = device(*m)
        pltpu.make_async_remote_copy(
            src_ref=pieces.at[to[0]], dst_ref=buf.at[yl, core, PLACE[m[2]], grp],
            send_sem=s_send, recv_sem=(t_recv if m[3] else s_recv).at[m[2]],
            device_id=to, device_id_type=MESH,
        ).start()
    buf[yl, core, 0, grp] = pieces[grp]
    inputs[2].wait()
    form_onehot(order_ref, onehot)

    y_device = device(0, 0, 0, 1)
    other = 1 - yl

    def to_y(n, first, count):
        send(held(yl, first, count), y_send.at[n], y_recv.at[n], y_device)

    def to_core(n, y, first, count):
        send(held(y, first, count), c_send.at[n], c_recv.at[n], c_device)

    def from_core(n, y, first, count):
        wait(buf.at[y, 1 - core, pl.ds(first, count)], c_recv.at[n])

    def permute(d):
        permute_level(buf, PLACE[d], onehot, permuted, lax.rem(z - d + 8, 8), d == 0)

    def half(y, place, h):
        return buf.at[y, core, place, pl.ds(4 * h, 4)]

    def relay(h, y, o, steps):
        for n in steps:
            n_sem, to = 3 * h + n - 1, device(0, 0, n if h == 0 else 8 - n)
            if n == 3:
                src, dst = half(y, 1 + h, h), half(y, 7, h)
            else:
                src, dst = held(y, 1 + h), held(y, 1 + h + 2 * n)
            send(src, r_send.at[o, n_sem], r_recv.at[o, n_sem], to, dst)

    def relayed(y, o, n):
        for h in range(2):
            dst = half(y, 7, h) if n == 3 else held(y, 1 + h + 2 * n)
            wait(dst, r_recv.at[o, 3 * h + n - 1])

    for h, d in enumerate((1, 7)):
        wait(held(yl, 1 + h), s_recv.at[d])
        relay(h, yl, 0, (1, 2, 3))
    for h, d in enumerate((1, 7)):
        wait(held(other, 1 + h), t_recv.at[d])
        relay(h, other, 1, (2, 3))
    wait(buf.at[yl, core, 0, pl.ds(0, 7)], s_recv.at[0])
    to_core(0, yl, 0, 3)
    wait(held(other, 0), t_recv.at[0])
    to_core(1, other, 0, 3)
    relayed(yl, 0, 1)
    to_y(0, 3, 2)
    to_core(2, yl, 3, 2)
    from_core(0, yl, 0, 3)
    from_core(1, other, 0, 3)
    for d in near:
        permute(d)
    left_rows(buf[pl.ds(yl, 1), pl.ds(core, 1), pl.ds(0, 1)].reshape(64, 128), rows, lhs)
    pltpu.make_async_copy(lhs, lhs_hbm, lhs_sem).start()
    relayed(yl, 0, 2)
    to_core(3, yl, 5, 2)
    wait(held(other, 3, 2), y_recv.at[0])
    to_core(4, other, 3, 2)
    relayed(yl, 0, 3)
    to_core(5, yl, 7, 1)
    relayed(other, 1, 2)
    to_core(6, other, 5, 2)
    relayed(other, 1, 3)
    to_core(7, other, 7, 1)
    from_core(2, yl, 3, 2)
    from_core(4, other, 3, 2)
    permute(2)
    permute(6)
    from_core(3, yl, 5, 2)
    from_core(6, other, 5, 2)
    permute(3)
    permute(5)
    from_core(5, yl, 7, 1)
    from_core(7, other, 7, 1)
    permute(4)
    weave_columns(permuted, cols, cols_hbm, cols_sem)
    for ref, s in sent:
        wait(ref, s)
    for n in range(len(direct) // 8):
        wait(buf.at[0, 0, 0], s_send)
    wait(buf.at[0, 0, 0, pl.ds(0, len(direct) % 8)], s_send)
    wait(lhs, lhs_sem)
    wait(cols, cols_sem)


def spectra_of_all(index, taps, order, volts):
    dma = pltpu.SemaphoreType.DMA
    vmem = pltpu.VMEM
    return pl.pallas_call(
        spectra_kernel,
        out_shape=[
            jax.ShapeDtypeStruct((512, 64), BF16),
            jax.ShapeDtypeStruct((64, 4096), BF16),
        ],
        in_specs=[pl.BlockSpec(memory_space=pltpu.HBM)] * 4,
        out_specs=[pl.BlockSpec(memory_space=pltpu.HBM)] * 2,
        scratch_shapes=[
            pltpu.SMEM((16,), I32),
            vmem((TAPS, NFFT), F32),
            vmem((16, 128), I32),
            vmem((FRAMES, 16, NFFT), BF16),
            vmem((FRAMES * 16, TAPS * 32), F32),
            vmem((8, 16, 128), F32),
            vmem((8, 8, 128), F32),
            vmem((2, 2, 8, 8, 8, 128), F32),
            vmem((8, 256, 2048), BF16),
            vmem((128, 2048), F32),
            vmem((256, 128), F32),
            vmem((512, 64), BF16),
            vmem((64, 4096), BF16),
            dma((3,)), dma((len(GROUPS),)), dma, dma,
            dma, dma((8,)), dma((8,)), dma((2, 6)), dma((2, 6)),
            dma((1,)), dma((1,)), dma((8,)), dma((8,)),
            *[vmem((TAPS * 32, FORM), BF16)] * (NFFT // FORM),
        ],
        compiler_params=pltpu.CompilerParams(
            collective_id=0, has_side_effects=True, vmem_limit_bytes=63 << 20
        ),
    )(index, taps, order, volts)


def correlate_kernel(lhs_hbm, cols_hbm, out_hbm, lhs, cols, out, lhs_sem, cols_sem, out_sem):
    steps = 4096 // QBLOCK
    left = pltpu.make_async_copy(lhs_hbm, lhs, lhs_sem)
    left.start()
    right = []
    for i in range(steps):
        at = pl.ds(i * QBLOCK, QBLOCK)
        right.append(pltpu.make_async_copy(cols_hbm.at[:, at], cols.at[:, at], cols_sem.at[i]))
        right[i].start()
    left.wait()
    for i in range(steps):
        at = pl.ds(i * QBLOCK, QBLOCK)
        right[i].wait()
        for c in range(2):
            x = jnp.dot(lhs[pl.ds(c * 256, 256), :], cols[:, at], preferred_element_type=F32)
            out[i, c] = x.astype(BF16).reshape(128, 2, QBLOCK)
            pltpu.make_async_copy(
                out.at[i, c], out_hbm.at[c, :, :, at], out_sem.at[i, c]
            ).start(priority=c)
    for i in range(steps):
        for c in range(2):
            pltpu.make_async_copy(out.at[i, c], out.at[i, c], out_sem.at[i, c]).wait()


def correlate(lhs, cols):
    dma = pltpu.SemaphoreType.DMA
    vmem = pltpu.VMEM
    return pl.pallas_call(
        correlate_kernel,
        out_shape=jax.ShapeDtypeStruct((2, 128, 2, 4096), BF16),
        in_specs=[pl.BlockSpec(memory_space=pltpu.HBM)] * 2,
        out_specs=pl.BlockSpec(memory_space=pltpu.HBM),
        scratch_shapes=[
            vmem((512, 64), BF16),
            vmem((64, 4096), BF16),
            vmem((4096 // QBLOCK, 2, 128, 2, QBLOCK), BF16),
            dma, dma((4096 // QBLOCK,)), dma((4096 // QBLOCK, 2)),
        ],
        compiler_params=pltpu.CompilerParams(vmem_limit_bytes=63 << 20),
    )(lhs, cols)


def per_device(voltages, filter_taps, channel_index, antenna_slot_order):
    lhs, cols = spectra_of_all(
        channel_index, filter_taps, antenna_slot_order.reshape(16, 128), voltages
    )
    return correlate(lhs, cols)


def solution(mesh):
    in_specs = (P(("blk", "grp"), None), P(), P(), P())
    out_specs = P("grp", "blk", None, None)
    return jax.shard_map(
        per_device, mesh=mesh, in_specs=in_specs, out_specs=out_specs, check_vma=False
    )
```
